32 devices in a mesh: row: 4 (over y, x), col: 8 (over z, core).
Axes of the slice: x: 2, y: 2, z: 4, core: 2. Of those that a mesh axis runs over, the one named last changes fastest.
Arguments:
- points: bfloat16 [2048, 768], P(('row', 'col')), may hold values from -8 to 8
- assign: int32 [2048], P(('row', 'col')), may hold values from 0 to 1023, as said below
Outputs:
- distance: float32 [2048, 1024], P('row', 'col')
The draws below stay inside these ranges and needn't reach their ends.
Inputs may be any that keep to these rules, and one draw needn't show every extreme that they name: Cluster group of a point is assign // 128. Among the 64 points of one device (aligned blocks of 64) at most 16 fall in one cluster group, and in every such block some group has exactly 16.
All inputs are finite; a program needn't handle non-finite values.
Results may differ from the reference program's by a relative error of at most 0.0003.
Values may be sent and summed in bfloat16 or wider, within the bound.
No kernel may reach another device: no remote copies, remote signals or barrier semaphores. Data moves between devices by JAX's collectives and lax.ppermute only.
A program may use at most 64 MiB of HBM per device.

```python
import jax
import jax.numpy as jnp
from jax import lax

D = 768
CL_DEV = 128
P_DEV = 64
SLOT = 16
CL = 1024
NPTS = 2048


def make_assign(key):
    key = jax.random.fold_in(key, 17)
    blocks = NPTS // P_DEV
    group_count = CL // CL_DEV
    pool_size = group_count * SLOT
    key_favor, key_score, key_forced, key_shuffle, key_local = jax.random.split(key, 5)
    favored = jax.random.randint(key_favor, (group_count,), 0, 2 ** 16)
    pool_group = jnp.arange(pool_size, dtype=jnp.int32) // SLOT
    scores = jax.random.randint(key_score, (blocks, pool_size), 0, 2 ** 16) + favored[pool_group][None, :]
    scores = scores * pool_size + jnp.arange(pool_size, dtype=jnp.int32)[None, :]
    forced = jax.random.randint(key_forced, (blocks,), 0, group_count)
    scores = jnp.where(pool_group[None, :] == forced[:, None], jnp.arange(pool_size, dtype=jnp.int32)[None, :] - 2 * pool_size, scores)
    chosen = jnp.argsort(scores, axis=1, stable=True)[:, :P_DEV]
    groups_drawn = chosen // SLOT
    shuffle_keys = jax.random.randint(key_shuffle, (blocks, P_DEV), 0, 2 ** 16) * P_DEV + jnp.arange(P_DEV, dtype=jnp.int32)[None, :]
    shuffle = jnp.argsort(shuffle_keys, axis=1, stable=True)
    groups_drawn = jnp.take_along_axis(groups_drawn, shuffle, axis=1)
    local_ids = jax.random.randint(key_local, (blocks, P_DEV), 0, CL_DEV)
    return (groups_drawn * CL_DEV + local_ids).reshape(NPTS).astype(jnp.int32)


def draw_assign(key, part=0):
    return make_assign(key)


def draw_points(key, part=0):
    assign = make_assign(key)
    key_centre = jax.random.fold_in(jax.random.fold_in(key, 29), 0)
    key_basis = jax.random.fold_in(jax.random.fold_in(key, 29), 2)
    key_latent = jax.random.fold_in(jax.random.fold_in(key, 29), 3)
    key_noise = jax.random.fold_in(jax.random.fold_in(key, 29), 4)
    latent_dims = 4
    latent_scale = 0.5
    noise_scale = 0.5
    basis = jax.random.normal(key_basis, (latent_dims, D), jnp.float32)
    centres = jax.random.normal(key_centre, (CL, D), jnp.float32)
    latent = jax.random.normal(key_latent, (NPTS, latent_dims), jnp.float32) * latent_scale
    noise = jax.random.normal(key_noise, (NPTS, D), jnp.float32) * noise_scale
    values = centres[assign] + jnp.dot(latent, basis) + noise
    return jnp.clip(values, -8.0, 8.0).astype(jnp.bfloat16)


def setup_inputs(seed: int = 0) -> dict:
    key_of = jax.random.split(jax.random.key(seed), 3)
    return {
        "points": draw_points(jax.random.fold_in(key_of[2], 71), 0),
        "assign": draw_assign(jax.random.fold_in(key_of[2], 71), 0),
    }


def squares(values):
    return jnp.sum(jnp.square(values.astype(jnp.float32)), axis=1)


def reference(points, assign):
    indicator = (assign[:, None] == jnp.arange(CL, dtype=jnp.int32)[None, :]).astype(jnp.bfloat16)
    norms = squares(points)
    block_rows = min(1024, NPTS)

    def block_sums(index):
        offset = (index * block_rows).astype(jnp.int32)
        part_rows = lax.dynamic_slice_in_dim(points, offset, block_rows, 0)
        part_norms = lax.dynamic_slice_in_dim(norms, offset, block_rows, 0)
        inner_prod = lax.dot_general(part_rows, points, (((1,), (1,)), ((), ())), preferred_element_type=jnp.float32)
        squared = part_norms[:, None] + norms[None, :] - 2.0 * inner_prod
        tile_vals = jnp.exp(-squared / D).astype(jnp.bfloat16)
        return jnp.dot(tile_vals, indicator, preferred_element_type=jnp.float32)

    row_sums = lax.map(block_sums, jnp.arange(NPTS // block_rows, dtype=jnp.int32)).reshape(NPTS, CL)
    weights = indicator.astype(jnp.float32)
    counts = jnp.sum(weights, axis=0)
    self_total = jnp.sum(weights * row_sums, axis=0)
    sizes_floor = jnp.maximum(counts, 1.0)
    return 1.0 - 2.0 * row_sums / sizes_floor[None, :] + self_total[None, :] / (sizes_floor * sizes_floor)[None, :]
```

```python
import functools

import jax
import jax.numpy as jnp
from jax import lax
from jax.experimental import pallas as pl
from jax.experimental.pallas import tpu as pltpu
from jax.sharding import PartitionSpec as P

CL_DEV = 128
ID_ROWS = 8
NT = (((1,), (1,)), ((), ()))
NN = (((1,), (0,)), ((), ()))


def dot(left, right, dims):
    return lax.dot_general(left, right, dims, preferred_element_type=jnp.float32)


def bucket_kernel(chips, slots, me_ref, assign_ref, points_ref, *payload_refs):
    own_count, width = points_ref.shape
    groups = 2 * chips
    total = groups * slots
    assign = assign_ref[...]
    group_of = assign // CL_DEV
    local_ids = assign - group_of * CL_DEV
    relative = group_of ^ me_ref[0]
    member = (
        lax.broadcasted_iota(jnp.int32, (groups, own_count), 0) == relative
    ).astype(jnp.float32)
    earlier = (
        lax.broadcasted_iota(jnp.int32, (own_count, own_count), 0)
        < lax.broadcasted_iota(jnp.int32, (own_count, own_count), 1)
    ).astype(jnp.bfloat16)
    rank = dot(member.astype(jnp.bfloat16), earlier, NN)
    position = jnp.sum(rank * member, axis=0, keepdims=True).astype(jnp.int32)
    half = chips * slots
    target = (relative & 1) * half + (relative >> 1) * slots + position
    dispatch = (
        lax.broadcasted_iota(jnp.int32, (total, own_count), 0) == target
    ).astype(jnp.bfloat16)
    rows = dot(dispatch, points_ref[...], NN).astype(jnp.bfloat16)
    ids = dot(
        jnp.broadcast_to(local_ids + 1, (ID_ROWS, own_count)).astype(jnp.bfloat16), dispatch, NT
    )
    lane = lax.broadcasted_iota(jnp.int32, (ID_ROWS, total), 1)
    owner = (lane % half) // slots
    for q, payload_ref in enumerate(payload_refs):
        for h in range(2):
            start = h * half + q * slots
            payload_ref[h * slots : (h + 1) * slots, :] = rows[start : start + slots]
        payload_ref[2 * slots :, :] = jnp.zeros((ID_ROWS, width), jnp.bfloat16)
        payload_ref[2 * slots :, :total] = jnp.where(owner == q, ids, 0.0).astype(jnp.bfloat16)


def merge_kernel(slots, *refs):
    *payload_refs, out_ref = refs
    half = len(payload_refs) * slots
    ids = jnp.zeros((ID_ROWS, out_ref.shape[1]), jnp.float32)
    for q, payload_ref in enumerate(payload_refs):
        for h in range(2):
            start = h * half + q * slots
            out_ref[start : start + slots, :] = payload_ref[h * slots : (h + 1) * slots, :]
        ids += payload_ref[2 * slots :, :].astype(jnp.float32)
    out_ref[2 * half :, :] = ids.astype(jnp.bfloat16)


def column_norms(rows):
    values = rows.astype(jnp.float32)
    return jnp.sum(values * values, axis=1, keepdims=True)


def row_of(column):
    return jnp.transpose(jnp.broadcast_to(column, (column.shape[0], 128)))[:1]


def distance_kernel(half, blocks, sets, chunk, me_ref, *refs):
    block_refs, set_refs = refs[:blocks], refs[blocks : blocks + sets]
    out_ref, rows_ref, slots_ref, norms_ref, hot_ref = refs[blocks + sets :]
    me = me_ref[0]
    own_count, width = block_refs[0].shape
    scale = 1.0 / width
    total = sets * half
    for s, set_ref in enumerate(set_refs):
        start = 0 if s < sets // 2 else half
        slot_rows = set_ref[start : start + half, :]
        slots_ref[s * half : (s + 1) * half, :] = slot_rows
        norms_ref[:, s * half : (s + 1) * half] = jnp.broadcast_to(
            row_of(column_norms(slot_rows)), (norms_ref.shape[0], half)
        )
        ids = set_ref[2 * half :, start : start + half].astype(jnp.float32)[:1]
        hot_ref[:, s * half : (s + 1) * half] = (
            lax.broadcasted_iota(jnp.int32, (CL_DEV, half), 0) + 1 == ids.astype(jnp.int32)
        ).astype(jnp.bfloat16)
    for b, block_ref in enumerate(block_refs):
        place = (me ^ (2 * b)) if b < blocks // 2 else (me ^ (2 * (b - blocks // 2)) ^ 1)
        rows_ref[pl.ds(pl.multiple_of(place * own_count, own_count), own_count), :] = block_ref[...]
    hot = hot_ref[...]
    slot_norms = norms_ref[:1, :]

    def kern(rows):
        inner = dot(rows, slots_ref[...], NT)
        squared = column_norms(rows) + slot_norms - 2.0 * inner
        return jnp.exp(squared * -scale).astype(jnp.bfloat16)

    ones = jnp.ones((8, total), jnp.bfloat16)
    sizes = jnp.maximum(dot(ones, hot, NT)[:1], 1.0)
    self_column = jnp.zeros((CL_DEV, 1), jnp.float32)
    for start in range(0, total, chunk):
        part = kern(slots_ref[start : start + chunk, :])
        weights = hot_ref[:, start : start + chunk]
        sums = dot(weights, part, NN)
        self_column += jnp.sum(sums * hot.astype(jnp.float32), axis=1, keepdims=True)
    self_total = row_of(self_column)
    offset = 1.0 + self_total / (sizes * sizes)
    factor = 2.0 / sizes
    for start in range(0, rows_ref.shape[0], chunk):
        row_sums = dot(kern(rows_ref[start : start + chunk, :]), hot, NT)
        out_ref[start : start + chunk, :] = offset - row_sums * factor


VMEM = pl.BlockSpec(memory_space=pltpu.VMEM)
SMEM = pl.BlockSpec(memory_space=pltpu.SMEM)


def per_device(points, assign):
    own_count, width = points.shape
    group_count, row_count = lax.axis_size("col"), lax.axis_size("row")
    chips = group_count // 2
    slots = max(2, 2 * own_count // group_count)
    half = chips * slots
    me = lax.axis_index("col").astype(jnp.int32).reshape(1)

    def over_col(values, bits):
        return lax.ppermute(values, "col", [(i, i ^ bits) for i in range(group_count)])

    def over_row(values, step):
        bit_count = row_count.bit_length() - 1
        pairs = []
        for r in range(row_count):
            for c in range(group_count):
                bit = step if c % 2 == 0 else bit_count - 1 - step
                pairs.append((r * group_count + c, (r ^ (1 << bit)) * group_count + c))
        return lax.ppermute(values, ("row", "col"), pairs)

    payloads = pl.pallas_call(
        functools.partial(bucket_kernel, chips, slots),
        out_shape=[jax.ShapeDtypeStruct((2 * slots + ID_ROWS, width), jnp.bfloat16)] * chips,
        in_specs=[SMEM, VMEM, VMEM],
        out_specs=[VMEM] * chips,
    )(me, assign.reshape(1, own_count), points)
    arrived = [payloads[0]] + [over_col(payloads[q], 2 * q) for q in range(1, chips)]
    blocks = [points] + [over_col(points, 2 * q) for q in range(1, chips)]
    sets = [
        pl.pallas_call(
            functools.partial(merge_kernel, slots),
            out_shape=jax.ShapeDtypeStruct((2 * half + ID_ROWS, width), jnp.bfloat16),
            in_specs=[VMEM] * chips,
            out_specs=VMEM,
        )(*arrived)
    ]
    step = 0
    while len(sets) < row_count:
        sets += [over_row(one, step) for one in sets]
        step += 1
    blocks += [over_col(one, 1) for one in blocks]
    sets += [over_col(one, 1) for one in sets]
    rows, total = len(blocks) * own_count, len(sets) * half
    chunk = min(256, rows)
    return pl.pallas_call(
        functools.partial(distance_kernel, half, len(blocks), len(sets), chunk),
        out_shape=jax.ShapeDtypeStruct((rows, CL_DEV), jnp.float32),
        in_specs=[SMEM] + [VMEM] * (len(blocks) + len(sets)),
        out_specs=VMEM,
        scratch_shapes=[
            pltpu.VMEM((rows, width), jnp.bfloat16),
            pltpu.VMEM((total, width), jnp.bfloat16),
            pltpu.VMEM((8, total), jnp.float32),
            pltpu.VMEM((CL_DEV, total), jnp.bfloat16),
        ],
        compiler_params=pltpu.CompilerParams(vmem_limit_bytes=32 * 1024 * 1024),
    )(me, *blocks, *sets)


def solution(mesh):
    return jax.shard_map(
        per_device,
        mesh=mesh,
        in_specs=(P(("row", "col"), None), P(("row", "col"))),
        out_specs=P("row", "col"),
        check_vma=False,
    )
```

```python
import functools

import jax
import jax.numpy as jnp
from jax import lax
from jax.experimental import pallas as pl
from jax.experimental.pallas import tpu as pltpu
from jax.sharding import PartitionSpec as P

CL_DEV = 128
ID_ROWS = 8
NT = (((1,), (1,)), ((), ()))
NN = (((1,), (0,)), ((), ()))
VMEM = pl.BlockSpec(memory_space=pltpu.VMEM)
MIB = 1024 * 1024


def dot(left, right, dims):
    return lax.dot_general(left, right, dims, preferred_element_type=jnp.float32)


def bf16(*shape):
    return jax.ShapeDtypeStruct(shape, jnp.bfloat16)


def call(kernel, out_shape, args, scratch=(), mib=8, after=(), cost=None):
    count = len(args)

    def body(*refs):
        kernel(*refs[:count], *refs[count + len(after) :])

    return pl.pallas_call(
        body,
        out_shape=out_shape,
        in_specs=[VMEM] * count + [pl.BlockSpec(memory_space=pl.ANY)] * len(after),
        out_specs=[VMEM] * len(out_shape),
        scratch_shapes=scratch,
        compiler_params=pltpu.CompilerParams(vmem_limit_bytes=mib * MIB),
        cost_estimate=cost,
    )(*args, *after)


def label_kernel(points_ref, labels_ref, out_ref):
    own_count, width = points_ref.shape
    out_ref[:own_count, :] = points_ref[...]
    out_ref[own_count:, :] = jnp.zeros((ID_ROWS, width), jnp.bfloat16)
    for n in range(2):
        out_ref[own_count:, n * CL_DEV : n * CL_DEV + own_count] = jnp.broadcast_to(
            labels_ref[n : n + 1, :].astype(jnp.float32), (ID_ROWS, own_count)
        ).astype(jnp.bfloat16)


def select_kernel(slots, *refs):
    *block_refs, local_ref, set_ref = refs
    count = len(block_refs)
    own_count = block_refs[0].shape[0] - ID_ROWS
    points = count * own_count
    half = count * slots
    me = lax.axis_index("col")
    earlier = (
        lax.broadcasted_iota(jnp.int32, (own_count, own_count), 0)
        < lax.broadcasted_iota(jnp.int32, (own_count, own_count), 1)
    ).astype(jnp.bfloat16)
    slot = lax.broadcasted_iota(jnp.int32, (2 * half, own_count), 0)
    ids = jnp.zeros((ID_ROWS, 2 * half), jnp.float32)
    dispatch = []
    for n, block_ref in enumerate(block_refs):
        local_ref[n * own_count : (n + 1) * own_count, :] = block_ref[:own_count, :]
        group_of = block_ref[own_count:, :own_count].astype(jnp.float32).astype(jnp.int32)
        labels = block_ref[own_count:, CL_DEV : CL_DEV + own_count].astype(jnp.float32) + 1.0
        relative = group_of ^ me
        member = lax.broadcasted_iota(jnp.int32, (ID_ROWS, own_count), 0) == relative
        rank = dot(member.astype(jnp.bfloat16), earlier, NN)
        position = jnp.sum(jnp.where(member, rank, 0.0), axis=0, keepdims=True)
        target = jnp.where(
            relative < 2, relative * half + n * slots + position.astype(jnp.int32), -1
        )
        chosen = (slot == target[:1]).astype(jnp.bfloat16)
        ids += dot(labels.astype(jnp.bfloat16), chosen, NT)
        dispatch.append(chosen)
    rows = dot(jnp.concatenate(dispatch, axis=1), local_ref[:points, :], NN).astype(jnp.bfloat16)
    for ref, start in ((local_ref, points), (set_ref, 0)):
        end = start + 2 * half
        ref[start:end, :] = rows
        ref[end:, :] = jnp.zeros((ID_ROWS, ref.shape[1]), jnp.bfloat16)
        ref[end:, : 2 * half] = ids.astype(jnp.bfloat16)


def column_norms(rows):
    values = rows.astype(jnp.float32)
    return jnp.sum(values * values, axis=1, keepdims=True)


def row_of(column):
    return jnp.transpose(jnp.broadcast_to(column, (column.shape[0], 128)))[:1]


class Half:
    def __init__(self, ref, base, count, second):
        self.ref, self.base, self.count = ref, base, count
        self.start = count if second else 0

    def rows(self):
        start = self.base + self.start
        return self.ref[start : start + self.count, :]

    def indicator(self):
        base = self.base + 2 * self.count
        ids = self.ref[base : base + ID_ROWS, self.start : self.start + self.count]
        ids = ids.astype(jnp.float32).astype(jnp.int32)[:1]
        clusters = lax.broadcasted_iota(jnp.int32, (CL_DEV, self.count), 0)
        return (clusters + 1 == ids).astype(jnp.bfloat16)


def stack_kernel(*refs):
    *in_refs, out_ref = refs
    place = 0
    for in_ref in in_refs:
        out_ref[place : place + in_ref.shape[0], :] = in_ref[...]
        place += in_ref.shape[0]


def stack(*arrays, after=()):
    rows = sum(one.shape[0] for one in arrays)
    return call(stack_kernel, [bf16(rows, arrays[0].shape[1])], arrays, after=after)[0]


def kern(rows, slots, slot_norms):
    inner = dot(rows, slots, NT)
    squared = column_norms(rows) + slot_norms - 2.0 * inner
    return jnp.exp(squared * (-1.0 / rows.shape[1])).astype(jnp.bfloat16)


def row_norms(slots_ref):
    pieces = [
        row_of(column_norms(slots_ref[start : start + CL_DEV, :]))
        for start in range(0, slots_ref.shape[0], CL_DEV)
    ]
    return jnp.concatenate(pieces, axis=1)


def chunks(begin, end, step):
    return [(start, min(start + step, end)) for start in range(begin, end, step)]


def sums_kernel(counts, parts, *refs):
    *array_refs, left_ref, hot_ref, sums_ref, totals_ref = refs
    rows, total = sums_ref.shape[0], left_ref.shape[0]
    place = 0
    for array_ref, count in zip(array_refs, counts):
        left_ref[place : place + count, :] = array_ref[:count, :]
        place += count
    for n, *rest in parts:
        part = Half(array_refs[n], *rest)
        end = place + part.count
        left_ref[place:end, :] = part.rows()
        hot_ref[:, place - rows : end - rows] = part.indicator()
        place = end
    slots, hot = left_ref[rows:, :], hot_ref[...]
    norms = row_norms(left_ref.at[rows:])
    for start, end in chunks(0, rows, 256):
        sums_ref[start:end, :] = dot(kern(left_ref[start:end, :], slots, norms), hot, NT)
    shares = jnp.zeros(hot.shape, jnp.float32)
    for start, end in chunks(rows, total, 256):
        tile = kern(left_ref[start:end, :], slots, norms)
        shares += dot(hot_ref[:, start - rows : end - rows], tile, NN)
    column = jnp.sum(shares * hot.astype(jnp.float32), axis=1, keepdims=True)
    ones = jnp.ones((8, total - rows), jnp.bfloat16)
    totals_ref[:8, :] = jnp.broadcast_to(row_of(column), (8, CL_DEV))
    totals_ref[8:, :] = dot(ones, hot, NT)


def distance_kernel(parts, order, *refs):
    left_ref, old_hot_ref, sums_ref, totals_ref, *refs = refs
    *array_refs, out_ref, slots_ref, hot_ref = refs
    rows, total = sums_ref.shape[0], left_ref.shape[0]
    place = 0
    for n, *rest in parts:
        part = Half(array_refs[n], *rest)
        end = place + part.count
        slots_ref[place:end, :] = part.rows()
        hot_ref[:, place:end] = part.indicator()
        place = end
    slots, hot = slots_ref[...], hot_ref[...]
    norms = row_norms(slots_ref)
    shares = dot(hot, kern(slots, slots, norms), NN)
    for start, end in chunks(rows, total, 512):
        tile = kern(left_ref[start:end, :], slots, norms)
        shares += 2.0 * dot(old_hot_ref[:, start - rows : end - rows], tile, NN)
    column = jnp.sum(shares * hot.astype(jnp.float32), axis=1, keepdims=True)
    totals = totals_ref[:1, :] + row_of(column)
    counts = totals_ref[8:9, :] + dot(jnp.ones((8, place), jnp.bfloat16), hot, NT)[:1]
    sizes = jnp.maximum(counts, 1.0)
    offset = 1.0 + totals / (sizes * sizes)
    factor = 2.0 / sizes
    me = lax.axis_index("col")
    own_count = rows // len(order)
    for start, end in chunks(0, rows, 512):
        part = sums_ref[start:end, :] + dot(kern(left_ref[start:end, :], slots, norms), hot, NT)
        part = offset - part * factor
        for b in range((end - start) // own_count):
            row = pl.multiple_of((me ^ order[start // own_count + b]) * own_count, own_count)
            out_ref[pl.ds(row, own_count), :] = part[b * own_count : (b + 1) * own_count]


def parts_of(sets, arrays):
    parts = []
    for one, base, count, second in sets:
        n = [array is one for array in arrays].index(True)
        for start in range(base, one.shape[0], 2 * count + ID_ROWS):
            parts.append((n, start, count, second))
    return parts


def cost_of(rows, slots, width):
    return pl.CostEstimate(
        flops=2 * rows * slots * (width + CL_DEV),
        bytes_accessed=2 * rows * width,
        transcendentals=rows * slots,
    )


def sum_slots(sets):
    arrays = [one for one, *_ in sets]
    counts = [base for _, base, *_ in sets if base]
    parts = parts_of(sets, arrays)
    width, rows, slots = arrays[0].shape[1], sum(counts), sum(part[2] for part in parts)
    return call(
        functools.partial(sums_kernel, counts, parts),
        [
            bf16(rows + slots, width),
            bf16(CL_DEV, slots),
            jax.ShapeDtypeStruct((rows, CL_DEV), jnp.float32),
            jax.ShapeDtypeStruct((16, CL_DEV), jnp.float32),
        ],
        arrays,
        mib=32,
        cost=cost_of(3 * (rows + slots), slots, width),
    )


def finish(order, sums, sets):
    arrays = [one for one, *_ in sets]
    parts = parts_of(sets, arrays)
    width, slots = arrays[0].shape[1], sum(part[2] for part in parts)
    return call(
        functools.partial(distance_kernel, parts, order),
        [jax.ShapeDtypeStruct(sums[2].shape, jnp.float32)],
        [*sums, *arrays],
        [pltpu.VMEM((slots, width), jnp.bfloat16), pltpu.VMEM((CL_DEV, slots), jnp.bfloat16)],
        mib=32,
        cost=cost_of(sums[0].shape[0] + slots, slots, width),
    )[0]


def per_device(points, assign):
    own_count, width = points.shape
    group_count, row_count = lax.axis_size("col"), lax.axis_size("row")
    chips = group_count // 2
    slots = max(2, 2 * own_count // group_count)

    def over_col(values, bits):
        return lax.ppermute(values, "col", [(i, i ^ bits) for i in range(group_count)])

    def over_row(values, bits_of):
        pairs = [
            (r * group_count + c, (r ^ bits_of(c)) * group_count + c)
            for r in range(row_count)
            for c in range(group_count)
        ]
        return lax.ppermute(values, ("row", "col"), pairs)

    def in_steps(sets, here):
        steps = row_count.bit_length() - 1
        for step in range(steps):
            got = over_row(sets, lambda c: 1 << (step if c % 2 == 0 else steps - 1 - step))
            if step < steps - 1:
                sets, here = stack(sets, got), stack(here, got)
        return here, got

    def at_once(sets, here):
        got = [over_row(sets, lambda c: bits) for bits in range(row_count - 1, 0, -1)]
        return here, stack(*got)

    group_of = assign // CL_DEV
    labels = jnp.stack([group_of, assign - group_of * CL_DEV])
    [labelled] = call(label_kernel, [bf16(own_count + ID_ROWS, width)], [points, labels])
    blocks = {0: labelled}
    bit = chips // 2
    while bit:
        blocks |= {q + bit: over_col(one, 2 * bit) for q, one in blocks.items()}
        bit //= 2
    places, near, last = [], [], []
    for batch, share in ((range(2), in_steps), (range(2, chips), at_once)):
        base, half = len(batch) * own_count, len(batch) * slots
        here, sets = call(
            functools.partial(select_kernel, slots),
            [bf16(base + 2 * half + ID_ROWS, width), bf16(2 * half + ID_ROWS, width)],
            [blocks[q] for q in batch],
            after=[one[0] for one in near],
        )
        here, got = share(sets, here)
        places.append([2 * q for q in batch])
        near.append((here, base, half))
        last.append((got, 0, half))

    def both_cores(one, base, half):
        return [(one, base, half, False), (over_col(one, 1), base, half, True)]

    pairs = [both_cores(*one) for one in near]
    old = [pair[0] for pair in pairs] + [pair[1] for pair in pairs] + both_cores(*last[0])
    order = [q for side in range(2) for batch in places for q in (one ^ side for one in batch)]
    sums = sum_slots(old)
    return finish(order, sums, both_cores(*last[1]))


def solution(mesh):
    return jax.shard_map(
        per_device,
        mesh=mesh,
        in_specs=(P(("row", "col"), None), P(("row", "col"))),
        out_specs=P("row", "col"),
        check_vma=False,
    )
```

```python
import functools

import jax
import jax.numpy as jnp
from jax import lax
from jax.experimental import pallas as pl
from jax.experimental.pallas import tpu as pltpu
from jax.sharding import PartitionSpec as P

CL_DEV = 128
ID_ROWS = 8
NT = (((1,), (1,)), ((), ()))
NN = (((1,), (0,)), ((), ()))
VMEM = pl.BlockSpec(memory_space=pltpu.VMEM)
MIB = 1024 * 1024


def dot(left, right, dims):
    return lax.dot_general(left, right, dims, preferred_element_type=jnp.float32)


def bf16(*shape):
    return jax.ShapeDtypeStruct(shape, jnp.bfloat16)


def call(kernel, out_shape, args, scratch=(), mib=8, after=(), cost=None):
    count = len(args)

    def body(*refs):
        kernel(*refs[:count], *refs[count + len(after) :])

    return pl.pallas_call(
        body,
        out_shape=out_shape,
        in_specs=[VMEM] * count + [pl.BlockSpec(memory_space=pl.ANY)] * len(after),
        out_specs=[VMEM] * len(out_shape),
        scratch_shapes=scratch,
        compiler_params=pltpu.CompilerParams(vmem_limit_bytes=mib * MIB),
        cost_estimate=cost,
    )(*args, *after)


def label_kernel(points_ref, assign_ref, out_ref):
    own_count, width = points_ref.shape
    assign = assign_ref[...]
    group_of = assign // CL_DEV
    out_ref[:own_count, :] = points_ref[...]
    out_ref[own_count:, :] = jnp.zeros((ID_ROWS, width), jnp.bfloat16)
    for start, labels in ((0, group_of), (CL_DEV, assign - group_of * CL_DEV)):
        out_ref[own_count:, start : start + own_count] = jnp.broadcast_to(
            labels.astype(jnp.float32), (ID_ROWS, own_count)
        ).astype(jnp.bfloat16)


def select_kernel(slots, *refs):
    *block_refs, local_ref, set_ref = refs
    count = len(block_refs)
    own_count = block_refs[0].shape[0] - ID_ROWS
    points = count * own_count
    half = count * slots
    me = lax.axis_index("col")
    earlier = (
        lax.broadcasted_iota(jnp.int32, (own_count, own_count), 0)
        < lax.broadcasted_iota(jnp.int32, (own_count, own_count), 1)
    ).astype(jnp.bfloat16)
    slot = lax.broadcasted_iota(jnp.int32, (2 * half, own_count), 0)
    ids = jnp.zeros((ID_ROWS, 2 * half), jnp.float32)
    dispatch = []
    for n, block_ref in enumerate(block_refs):
        local_ref[n * own_count : (n + 1) * own_count, :] = block_ref[:own_count, :]
        group_of = block_ref[own_count:, :own_count].astype(jnp.float32).astype(jnp.int32)
        labels = block_ref[own_count:, CL_DEV : CL_DEV + own_count].astype(jnp.float32) + 1.0
        relative = group_of ^ me
        member = lax.broadcasted_iota(jnp.int32, (ID_ROWS, own_count), 0) == relative
        rank = dot(member.astype(jnp.bfloat16), earlier, NN)
        position = jnp.sum(jnp.where(member, rank, 0.0), axis=0, keepdims=True)
        target = jnp.where(
            relative < 2, relative * half + n * slots + position.astype(jnp.int32), -1
        )
        chosen = (slot == target[:1]).astype(jnp.bfloat16)
        ids += dot(labels.astype(jnp.bfloat16), chosen, NT)
        dispatch.append(chosen)
    rows = dot(jnp.concatenate(dispatch, axis=1), local_ref[:points, :], NN).astype(jnp.bfloat16)
    for ref, start in ((local_ref, points), (set_ref, 0)):
        end = start + 2 * half
        ref[start:end, :] = rows
        ref[end:, :] = jnp.zeros((ID_ROWS, ref.shape[1]), jnp.bfloat16)
        ref[end:, : 2 * half] = ids.astype(jnp.bfloat16)


def column_norms(rows):
    values = rows.astype(jnp.float32)
    return jnp.sum(values * values, axis=1, keepdims=True)


def row_of(column):
    return jnp.transpose(jnp.broadcast_to(column, (column.shape[0], 128)))[:1]


class Half:
    def __init__(self, ref, base, count, second):
        self.ref, self.base, self.count = ref, base, count
        self.start = count if second else 0

    def rows(self):
        start = self.base + self.start
        return self.ref[start : start + self.count, :]

    def indicator(self):
        base = self.base + 2 * self.count
        ids = self.ref[base : base + ID_ROWS, self.start : self.start + self.count]
        ids = ids.astype(jnp.float32).astype(jnp.int32)[:1]
        clusters = lax.broadcasted_iota(jnp.int32, (CL_DEV, self.count), 0)
        return (clusters + 1 == ids).astype(jnp.bfloat16)


def stack_kernel(*refs):
    *in_refs, out_ref = refs
    place = 0
    for in_ref in in_refs:
        out_ref[place : place + in_ref.shape[0], :] = in_ref[...]
        place += in_ref.shape[0]


def stack(*arrays, after=(), cost=None):
    rows = sum(one.shape[0] for one in arrays)
    return call(stack_kernel, [bf16(rows, arrays[0].shape[1])], arrays, after=after, cost=cost)[0]


def kern(rows, slots, slot_norms):
    inner = dot(rows, slots, NT)
    squared = column_norms(rows) + slot_norms - 2.0 * inner
    return jnp.exp(squared * (-1.0 / rows.shape[1])).astype(jnp.bfloat16)


def row_norms(slots_ref):
    pieces = [
        row_of(column_norms(slots_ref[start : start + CL_DEV, :]))
        for start in range(0, slots_ref.shape[0], CL_DEV)
    ]
    return jnp.concatenate(pieces, axis=1)


def chunks(begin, end, step):
    return [(start, min(start + step, end)) for start in range(begin, end, step)]


def sums_kernel(counts, parts, *refs):
    *array_refs, left_ref, hot_ref, sums_ref, totals_ref = refs
    rows, total = sums_ref.shape[0], left_ref.shape[0]
    place = 0
    for array_ref, count in zip(array_refs, counts):
        left_ref[place : place + count, :] = array_ref[:count, :]
        place += count
    for n, *rest in parts:
        part = Half(array_refs[n], *rest)
        end = place + part.count
        left_ref[place:end, :] = part.rows()
        hot_ref[:, place - rows : end - rows] = part.indicator()
        place = end
    slots, hot = left_ref[rows:, :], hot_ref[...]
    norms = row_norms(left_ref.at[rows:])
    for start, end in chunks(0, rows, 256):
        sums_ref[start:end, :] = dot(kern(left_ref[start:end, :], slots, norms), hot, NT)
    shares = jnp.zeros(hot.shape, jnp.float32)
    for start, end in chunks(rows, total, 256):
        tile = kern(left_ref[start:end, :], slots, norms)
        shares += dot(hot_ref[:, start - rows : end - rows], tile, NN)
    column = jnp.sum(shares * hot.astype(jnp.float32), axis=1, keepdims=True)
    ones = jnp.ones((8, total - rows), jnp.bfloat16)
    totals_ref[:8, :] = jnp.broadcast_to(row_of(column), (8, CL_DEV))
    totals_ref[8:, :] = dot(ones, hot, NT)


def distance_kernel(parts, order, *refs):
    left_ref, old_hot_ref, sums_ref, totals_ref, *refs = refs
    *array_refs, out_ref, slots_ref, hot_ref = refs
    rows, total = sums_ref.shape[0], left_ref.shape[0]
    place = 0
    for n, *rest in parts:
        part = Half(array_refs[n], *rest)
        end = place + part.count
        slots_ref[place:end, :] = part.rows()
        hot_ref[:, place:end] = part.indicator()
        place = end
    slots, hot = slots_ref[...], hot_ref[...]
    norms = row_norms(slots_ref)
    shares = dot(hot, kern(slots, slots, norms), NN)
    for start, end in chunks(rows, total, 512):
        tile = kern(left_ref[start:end, :], slots, norms)
        shares += 2.0 * dot(old_hot_ref[:, start - rows : end - rows], tile, NN)
    column = jnp.sum(shares * hot.astype(jnp.float32), axis=1, keepdims=True)
    totals = totals_ref[:1, :] + row_of(column)
    counts = totals_ref[8:9, :] + dot(jnp.ones((8, place), jnp.bfloat16), hot, NT)[:1]
    sizes = jnp.maximum(counts, 1.0)
    offset = 1.0 + totals / (sizes * sizes)
    factor = 2.0 / sizes
    me = lax.axis_index("col")
    own_count = rows // len(order)
    for start, end in chunks(0, rows, 512):
        part = sums_ref[start:end, :] + dot(kern(left_ref[start:end, :], slots, norms), hot, NT)
        part = offset - part * factor
        for b in range((end - start) // own_count):
            row = pl.multiple_of((me ^ order[start // own_count + b]) * own_count, own_count)
            out_ref[pl.ds(row, own_count), :] = part[b * own_count : (b + 1) * own_count]


def parts_of(sets, arrays):
    parts = []
    for one, base, count, second in sets:
        n = [array is one for array in arrays].index(True)
        for start in range(base, one.shape[0], 2 * count + ID_ROWS):
            parts.append((n, start, count, second))
    return parts


def cost_of(rows, slots, width):
    return pl.CostEstimate(
        flops=2 * rows * slots * (width + CL_DEV),
        bytes_accessed=2 * rows * width,
        transcendentals=rows * slots,
    )


def sum_slots(sets):
    arrays = [one for one, *_ in sets]
    counts = [base for _, base, *_ in sets if base]
    parts = parts_of(sets, arrays)
    width, rows, slots = arrays[0].shape[1], sum(counts), sum(part[2] for part in parts)
    return call(
        functools.partial(sums_kernel, counts, parts),
        [
            bf16(rows + slots, width),
            bf16(CL_DEV, slots),
            jax.ShapeDtypeStruct((rows, CL_DEV), jnp.float32),
            jax.ShapeDtypeStruct((16, CL_DEV), jnp.float32),
        ],
        arrays,
        mib=32,
        cost=cost_of(1 * (rows + slots), slots, width),
    )


def finish(order, sums, sets):
    arrays = [one for one, *_ in sets]
    parts = parts_of(sets, arrays)
    width, slots = arrays[0].shape[1], sum(part[2] for part in parts)
    return call(
        functools.partial(distance_kernel, parts, order),
        [jax.ShapeDtypeStruct(sums[2].shape, jnp.float32)],
        [*sums, *arrays],
        [pltpu.VMEM((slots, width), jnp.bfloat16), pltpu.VMEM((CL_DEV, slots), jnp.bfloat16)],
        mib=32,
        cost=cost_of(sums[0].shape[0] + slots, slots, width),
    )[0]


def per_device(points, assign):
    own_count, width = points.shape
    group_count, row_count = lax.axis_size("col"), lax.axis_size("row")
    chips = group_count // 2
    slots = max(2, 2 * own_count // group_count)

    def over_col(values, bits):
        return lax.ppermute(values, "col", [(i, i ^ bits) for i in range(group_count)])

    def over_row(values, bits):
        return lax.ppermute(values, "row", [(i, i ^ bits) for i in range(row_count)])

    def pending(one, flops):
        return stack(one, cost=pl.CostEstimate(flops=int(flops), bytes_accessed=0, transcendentals=0))

    def label(values, ids):
        return call(label_kernel, [bf16(own_count + ID_ROWS, width)], [values, ids])[0]

    assign = assign.reshape(1, own_count)
    far = chips // 2
    blocks = {0: label(points, assign)}
    for q in sorted({far, 1}, reverse=True):
        blocks[q] = label(pending(over_col(points, 2 * q), 1e8 if q > 1 else 4e9), over_col(assign, 2 * q))
    bit = far // 2
    while bit:
        for q in range(0, chips, 2 * bit):
            if q + bit not in blocks:
                blocks[q + bit] = pending(over_col(blocks[q], 2 * bit), 1e9)
        bit //= 2
    places, near, last = [], [], []
    for batch in (range(2), range(2, chips)):
        base, half = len(batch) * own_count, len(batch) * slots
        here, sets = call(
            functools.partial(select_kernel, slots),
            [bf16(base + 2 * half + ID_ROWS, width), bf16(2 * half + ID_ROWS, width)],
            [blocks[q] for q in batch],
            after=[] if last else [blocks[far]],
        )
        got = [over_row(sets, bits) for bits in range(row_count - 1, 0, -1)]
        places.append([2 * q for q in batch])
        near.append((here, base, half))
        last.append((got, 0, half))

    def both_cores(one, base, half):
        return [(one, base, half, False), (over_col(one, 1), base, half, True)]

    pairs = [both_cores(*one) for one in near]
    got, base, half = last[0]
    first = both_cores(stack(*got), base, half)
    old = [pair[0] for pair in pairs] + [pair[1] for pair in pairs] + first
    order = [q for side in range(2) for batch in places for q in (one ^ side for one in batch)]
    sums = sum_slots(old)
    got, base, half = last[1]
    return finish(order, sums, both_cores(stack(*got), base, half))


def solution(mesh):
    return jax.shard_map(
        per_device,
        mesh=mesh,
        in_specs=(P(("row", "col"), None), P(("row", "col"))),
        out_specs=P("row", "col"),
        check_vma=False,
    )
```

```python
import functools

import jax
import jax.numpy as jnp
from jax import lax
from jax.experimental import pallas as pl
from jax.experimental.pallas import tpu as pltpu
from jax.sharding import PartitionSpec as P

CL_DEV = 128
ID_ROWS = 8
LANES = 128
NT = (((1,), (1,)), ((), ()))
NN = (((1,), (0,)), ((), ()))
VMEM = pl.BlockSpec(memory_space=pltpu.VMEM)
MIB = 1024 * 1024


def dot(left, right, dims):
    return lax.dot_general(left, right, dims, preferred_element_type=jnp.float32)


def bf16(*shape):
    return jax.ShapeDtypeStruct(shape, jnp.bfloat16)


def call(kernel, out_shape, args, scratch=(), mib=8, after=(), cost=None):
    count = len(args)

    def body(*refs):
        kernel(*refs[:count], *refs[count + len(after) :])

    return pl.pallas_call(
        body,
        out_shape=out_shape,
        in_specs=[VMEM] * count + [pl.BlockSpec(memory_space=pl.ANY)] * len(after),
        out_specs=[VMEM] * len(out_shape),
        scratch_shapes=scratch,
        compiler_params=pltpu.CompilerParams(vmem_limit_bytes=mib * MIB),
        cost_estimate=cost,
    )(*args, *after)


def tall(rows):
    return [rows[:, start : start + LANES] for start in range(0, rows.shape[1], LANES)]


def put_tall(ref, base, rows):
    count = rows.shape[0]
    for t, piece in enumerate(tall(rows)):
        ref[base + t * count : base + (t + 1) * count, :] = piece


def label_kernel(points_ref, assign_ref, out_ref):
    own_count = points_ref.shape[0]
    assign = assign_ref[...]
    group_of = assign // CL_DEV
    put_tall(out_ref, 0, points_ref[...])
    end = out_ref.shape[0] - ID_ROWS
    out_ref[end:, :] = jnp.zeros((ID_ROWS, LANES), jnp.bfloat16)
    for n, labels in enumerate((group_of, assign - group_of * CL_DEV)):
        out_ref[end:, n * own_count : (n + 1) * own_count] = jnp.broadcast_to(
            labels.astype(jnp.float32), (ID_ROWS, own_count)
        ).astype(jnp.bfloat16)


def select_kernel(slots, *refs):
    *block_refs, local_ref, set_ref, points_ref = refs
    count = len(block_refs)
    points, width = points_ref.shape
    own_count = points // count
    half = count * slots
    me = lax.axis_index("col")
    earlier = (
        lax.broadcasted_iota(jnp.int32, (own_count, own_count), 0)
        < lax.broadcasted_iota(jnp.int32, (own_count, own_count), 1)
    ).astype(jnp.bfloat16)
    slot = lax.broadcasted_iota(jnp.int32, (2 * half, own_count), 0)
    ids = jnp.zeros((ID_ROWS, 2 * half), jnp.float32)
    dispatch = []
    for n, block_ref in enumerate(block_refs):
        for t in range(width // LANES):
            points_ref[n * own_count : (n + 1) * own_count, t * LANES : (t + 1) * LANES] = block_ref[
                t * own_count : (t + 1) * own_count, :
            ]
        end = block_ref.shape[0] - ID_ROWS
        group_of = block_ref[end:, :own_count].astype(jnp.float32).astype(jnp.int32)
        labels = block_ref[end:, own_count : 2 * own_count].astype(jnp.float32) + 1.0
        relative = group_of ^ me
        member = lax.broadcasted_iota(jnp.int32, (ID_ROWS, own_count), 0) == relative
        rank = dot(member.astype(jnp.bfloat16), earlier, NN)
        position = jnp.sum(jnp.where(member, rank, 0.0), axis=0, keepdims=True)
        target = jnp.where(
            relative < 2, relative * half + n * slots + position.astype(jnp.int32), -1
        )
        chosen = (slot == target[:1]).astype(jnp.bfloat16)
        ids += dot(labels.astype(jnp.bfloat16), chosen, NT)
        dispatch.append(chosen)
    rows = dot(jnp.concatenate(dispatch, axis=1), points_ref[...], NN).astype(jnp.bfloat16)
    put_tall(local_ref, 0, points_ref[...])
    for ref, start in ((local_ref, points * width // LANES), (set_ref, 0)):
        end = ref.shape[0] - ID_ROWS
        put_tall(ref, start, rows)
        ref[end:, :] = jnp.zeros((ID_ROWS, LANES), jnp.bfloat16)
        ref[end:, : 2 * half] = ids.astype(jnp.bfloat16)


def column_norms(rows):
    values = rows.astype(jnp.float32)
    return jnp.sum(values * values, axis=1, keepdims=True)


def row_of(column):
    return jnp.transpose(jnp.broadcast_to(column, (column.shape[0], 128)))[:1]


class Half:
    def __init__(self, ref, base, count, second):
        self.ref, self.base, self.count = ref, base, count
        self.start = count if second else 0

    def put(self, out_ref, place):
        for t in range(out_ref.shape[1] // LANES):
            start = self.base + 2 * t * self.count + self.start
            out_ref[place : place + self.count, t * LANES : (t + 1) * LANES] = self.ref[
                start : start + self.count, :
            ]

    def indicator(self, width):
        base = self.base + 2 * self.count * width // LANES
        ids = self.ref[base : base + ID_ROWS, self.start : self.start + self.count]
        ids = ids.astype(jnp.float32).astype(jnp.int32)[:1]
        clusters = lax.broadcasted_iota(jnp.int32, (CL_DEV, self.count), 0)
        return (clusters + 1 == ids).astype(jnp.bfloat16)


def stack_kernel(*refs):
    *in_refs, out_ref = refs
    place = 0
    for in_ref in in_refs:
        out_ref[place : place + in_ref.shape[0], :] = in_ref[...]
        place += in_ref.shape[0]


def stack(*arrays, after=(), cost=None):
    rows = sum(one.shape[0] for one in arrays)
    return call(stack_kernel, [bf16(rows, arrays[0].shape[1])], arrays, after=after, cost=cost)[0]


def kern(rows, slots, slot_norms):
    inner = dot(rows, slots, NT)
    squared = column_norms(rows) + slot_norms - 2.0 * inner
    return jnp.exp(squared * (-1.0 / rows.shape[1])).astype(jnp.bfloat16)


def row_norms(slots_ref):
    pieces = [
        row_of(column_norms(slots_ref[start : start + CL_DEV, :]))
        for start in range(0, slots_ref.shape[0], CL_DEV)
    ]
    return jnp.concatenate(pieces, axis=1)


def chunks(begin, end, step):
    return [(start, min(start + step, end)) for start in range(begin, end, step)]


def sums_kernel(counts, parts, *refs):
    *array_refs, left_ref, hot_ref, sums_ref, totals_ref = refs
    rows, (total, width) = sums_ref.shape[0], left_ref.shape
    place = 0
    for array_ref, count in zip(array_refs, counts):
        for t in range(width // LANES):
            left_ref[place : place + count, t * LANES : (t + 1) * LANES] = array_ref[
                t * count : (t + 1) * count, :
            ]
        place += count
    for n, *rest in parts:
        part = Half(array_refs[n], *rest)
        end = place + part.count
        part.put(left_ref, place)
        hot_ref[:, place - rows : end - rows] = part.indicator(width)
        place = end
    slots, hot = left_ref[rows:, :], hot_ref[...]
    norms = row_norms(left_ref.at[rows:])
    for start, end in chunks(0, rows, 256):
        sums_ref[start:end, :] = dot(kern(left_ref[start:end, :], slots, norms), hot, NT)
    shares = jnp.zeros(hot.shape, jnp.float32)
    for start, end in chunks(rows, total, 256):
        tile = kern(left_ref[start:end, :], slots, norms)
        shares += dot(hot_ref[:, start - rows : end - rows], tile, NN)
    column = jnp.sum(shares * hot.astype(jnp.float32), axis=1, keepdims=True)
    ones = jnp.ones((8, total - rows), jnp.bfloat16)
    totals_ref[:8, :] = jnp.broadcast_to(row_of(column), (8, CL_DEV))
    totals_ref[8:, :] = dot(ones, hot, NT)


def distance_kernel(parts, order, *refs):
    left_ref, old_hot_ref, sums_ref, totals_ref, *refs = refs
    *array_refs, out_ref, slots_ref, hot_ref = refs
    rows, total = sums_ref.shape[0], left_ref.shape[0]
    place = 0
    for n, *rest in parts:
        part = Half(array_refs[n], *rest)
        end = place + part.count
        part.put(slots_ref, place)
        hot_ref[:, place:end] = part.indicator(slots_ref.shape[1])
        place = end
    slots, hot = slots_ref[...], hot_ref[...]
    norms = row_norms(slots_ref)
    shares = dot(hot, kern(slots, slots, norms), NN)
    for start, end in chunks(rows, total, 512):
        tile = kern(left_ref[start:end, :], slots, norms)
        shares += 2.0 * dot(old_hot_ref[:, start - rows : end - rows], tile, NN)
    column = jnp.sum(shares * hot.astype(jnp.float32), axis=1, keepdims=True)
    totals = totals_ref[:1, :] + row_of(column)
    counts = totals_ref[8:9, :] + dot(jnp.ones((8, place), jnp.bfloat16), hot, NT)[:1]
    sizes = jnp.maximum(counts, 1.0)
    offset = 1.0 + totals / (sizes * sizes)
    factor = 2.0 / sizes
    me = lax.axis_index("col")
    own_count = rows // len(order)
    for start, end in chunks(0, rows, 512):
        part = sums_ref[start:end, :] + dot(kern(left_ref[start:end, :], slots, norms), hot, NT)
        part = offset - part * factor
        for b in range((end - start) // own_count):
            row = pl.multiple_of((me ^ order[start // own_count + b]) * own_count, own_count)
            out_ref[pl.ds(row, own_count), :] = part[b * own_count : (b + 1) * own_count]


def parts_of(sets, arrays, width):
    parts = []
    for one, base, count, second in sets:
        n = [array is one for array in arrays].index(True)
        for start in range(base, one.shape[0], 2 * count * width // LANES + ID_ROWS):
            parts.append((n, start, count, second))
    return parts


def cost_of(rows, slots, width):
    return pl.CostEstimate(
        flops=2 * rows * slots * (width + CL_DEV),
        bytes_accessed=2 * rows * width,
        transcendentals=rows * slots,
    )


def sum_slots(sets, width):
    arrays = [one for one, *_ in sets]
    counts = [base * LANES // width for _, base, *_ in sets if base]
    parts = parts_of(sets, arrays, width)
    rows, slots = sum(counts), sum(part[2] for part in parts)
    return call(
        functools.partial(sums_kernel, counts, parts),
        [
            bf16(rows + slots, width),
            bf16(CL_DEV, slots),
            jax.ShapeDtypeStruct((rows, CL_DEV), jnp.float32),
            jax.ShapeDtypeStruct((16, CL_DEV), jnp.float32),
        ],
        arrays,
        mib=32,
        cost=cost_of(1 * (rows + slots), slots, width),
    )


def finish(order, sums, sets, width):
    arrays = [one for one, *_ in sets]
    parts = parts_of(sets, arrays, width)
    slots = sum(part[2] for part in parts)
    return call(
        functools.partial(distance_kernel, parts, order),
        [jax.ShapeDtypeStruct(sums[2].shape, jnp.float32)],
        [*sums, *arrays],
        [pltpu.VMEM((slots, width), jnp.bfloat16), pltpu.VMEM((CL_DEV, slots), jnp.bfloat16)],
        mib=32,
        cost=cost_of(sums[0].shape[0] + slots, slots, width),
    )[0]


def per_device(points, assign):
    own_count, width = points.shape
    group_count, row_count = lax.axis_size("col"), lax.axis_size("row")
    chips, tiles = group_count // 2, width // LANES
    slots = max(2, 2 * own_count // group_count)

    def over_col(values, bits):
        return lax.ppermute(values, "col", [(i, i ^ bits) for i in range(group_count)])

    def over_row(values, bits):
        return lax.ppermute(values, "row", [(i, i ^ bits) for i in range(row_count)])

    def pending(one, flops):
        return stack(one, cost=pl.CostEstimate(flops=int(flops), bytes_accessed=0, transcendentals=0))

    def label(values, ids):
        return call(label_kernel, [bf16(own_count * tiles + ID_ROWS, LANES)], [values, ids])[0]

    assign = assign.reshape(1, own_count)
    far = chips // 2
    blocks = {0: label(points, assign)}
    for q in sorted({far, 1}, reverse=True):
        blocks[q] = label(pending(over_col(points, 2 * q), 1e8 if q > 1 else 4e9), over_col(assign, 2 * q))
    bit = far // 2
    while bit:
        for q in range(0, chips, 2 * bit):
            if q + bit not in blocks:
                blocks[q + bit] = pending(over_col(blocks[q], 2 * bit), 1e9)
        bit //= 2
    places, near, last = [], [], []
    for batch in (range(2), range(2, chips)):
        base, half = len(batch) * own_count * tiles, len(batch) * slots
        set_rows = 2 * half * tiles + ID_ROWS
        here, sets = call(
            functools.partial(select_kernel, slots),
            [bf16(base + set_rows, LANES), bf16(set_rows, LANES)],
            [blocks[q] for q in batch],
            [pltpu.VMEM((len(batch) * own_count, width), jnp.bfloat16)],
            after=[] if last else [blocks[far]],
        )
        got = [over_row(sets, bits) for bits in range(row_count - 1, 0, -1)]
        places.append([2 * q for q in batch])
        near.append((here, base, half))
        last.append((got, 0, half))

    def both_cores(one, base, half):
        return [(one, base, half, False), (over_col(one, 1), base, half, True)]

    pairs = [both_cores(*one) for one in near]
    got, base, half = last[0]
    first = both_cores(stack(*got), base, half)
    old = [pair[0] for pair in pairs] + [pair[1] for pair in pairs] + first
    order = [q for side in range(2) for batch in places for q in (one ^ side for one in batch)]
    sums = sum_slots(old, width)
    got, base, half = last[1]
    return finish(order, sums, both_cores(stack(*got), base, half), width)


def solution(mesh):
    return jax.shard_map(
        per_device,
        mesh=mesh,
        in_specs=(P(("row", "col"), None), P(("row", "col"))),
        out_specs=P("row", "col"),
        check_vma=False,
    )
```

```python
import functools

import jax
import jax.numpy as jnp
from jax import lax
from jax.experimental import pallas as pl
from jax.experimental.pallas import tpu as pltpu
from jax.sharding import PartitionSpec as P

CL_DEV = 128
ID_ROWS = 8
LANES = 128
NT = (((1,), (1,)), ((), ()))
NN = (((1,), (0,)), ((), ()))
VMEM = pl.BlockSpec(memory_space=pltpu.VMEM)
MIB = 1024 * 1024


def dot(left, right, dims):
    return lax.dot_general(left, right, dims, preferred_element_type=jnp.float32)


def bf16(*shape):
    return jax.ShapeDtypeStruct(shape, jnp.bfloat16)


def call(kernel, out_shape, args, scratch=(), mib=8, after=(), cost=None):
    count = len(args)

    def body(*refs):
        kernel(*refs[:count], *refs[count + len(after) :])

    return pl.pallas_call(
        body,
        out_shape=out_shape,
        in_specs=[VMEM] * count + [pl.BlockSpec(memory_space=pl.ANY)] * len(after),
        out_specs=[VMEM] * len(out_shape),
        scratch_shapes=scratch,
        compiler_params=pltpu.CompilerParams(vmem_limit_bytes=mib * MIB),
        cost_estimate=cost,
    )(*args, *after)


def tall(rows):
    return [rows[:, start : start + LANES] for start in range(0, rows.shape[1], LANES)]


def put_tall(ref, base, rows):
    count = rows.shape[0]
    for t, piece in enumerate(tall(rows)):
        ref[base + t * count : base + (t + 1) * count, :] = piece


def label_kernel(points_ref, assign_ref, out_ref):
    own_count = points_ref.shape[0]
    assign = assign_ref[...]
    group_of = assign // CL_DEV
    put_tall(out_ref, 0, points_ref[...])
    end = out_ref.shape[0] - ID_ROWS
    out_ref[end:, :] = jnp.zeros((ID_ROWS, LANES), jnp.bfloat16)
    for n, labels in enumerate((group_of, assign - group_of * CL_DEV)):
        out_ref[end:, n * own_count : (n + 1) * own_count] = jnp.broadcast_to(
            labels.astype(jnp.float32), (ID_ROWS, own_count)
        ).astype(jnp.bfloat16)


def select_kernel(slots, *refs):
    *block_refs, local_ref, set_ref, points_ref = refs
    count = len(block_refs)
    points, width = points_ref.shape
    own_count = points // count
    half = count * slots
    me = lax.axis_index("col")
    earlier = (
        lax.broadcasted_iota(jnp.int32, (own_count, own_count), 0)
        < lax.broadcasted_iota(jnp.int32, (own_count, own_count), 1)
    ).astype(jnp.bfloat16)
    slot = lax.broadcasted_iota(jnp.int32, (2 * half, own_count), 0)
    ids = jnp.zeros((ID_ROWS, 2 * half), jnp.float32)
    dispatch = []
    for n, block_ref in enumerate(block_refs):
        for t in range(width // LANES):
            points_ref[n * own_count : (n + 1) * own_count, t * LANES : (t + 1) * LANES] = block_ref[
                t * own_count : (t + 1) * own_count, :
            ]
        end = block_ref.shape[0] - ID_ROWS
        group_of = block_ref[end:, :own_count].astype(jnp.float32).astype(jnp.int32)
        labels = block_ref[end:, own_count : 2 * own_count].astype(jnp.float32) + 1.0
        relative = group_of ^ me
        member = lax.broadcasted_iota(jnp.int32, (ID_ROWS, own_count), 0) == relative
        rank = dot(member.astype(jnp.bfloat16), earlier, NN)
        position = jnp.sum(jnp.where(member, rank, 0.0), axis=0, keepdims=True)
        target = jnp.where(
            relative < 2, relative * half + n * slots + position.astype(jnp.int32), -1
        )
        chosen = (slot == target[:1]).astype(jnp.bfloat16)
        ids += dot(labels.astype(jnp.bfloat16), chosen, NT)
        dispatch.append(chosen)
    rows = dot(jnp.concatenate(dispatch, axis=1), points_ref[...], NN).astype(jnp.bfloat16)
    put_tall(local_ref, 0, points_ref[...])
    for ref, start in ((local_ref, points * width // LANES), (set_ref, 0)):
        end = ref.shape[0] - ID_ROWS
        put_tall(ref, start, rows)
        ref[end:, :] = jnp.zeros((ID_ROWS, LANES), jnp.bfloat16)
        ref[end:, : 2 * half] = ids.astype(jnp.bfloat16)


def column_norms(rows):
    values = rows.astype(jnp.float32)
    return jnp.sum(values * values, axis=1, keepdims=True)


def row_of(column):
    return jnp.transpose(jnp.broadcast_to(column, (column.shape[0], 128)))[:1]


class Half:
    def __init__(self, ref, base, count, second):
        self.ref, self.base, self.count = ref, base, count
        self.start = count if second else 0

    def put(self, out_ref, place):
        for t in range(out_ref.shape[1] // LANES):
            start = self.base + 2 * t * self.count + self.start
            out_ref[place : place + self.count, t * LANES : (t + 1) * LANES] = self.ref[
                start : start + self.count, :
            ]

    def indicator(self, width):
        base = self.base + 2 * self.count * width // LANES
        ids = self.ref[base : base + ID_ROWS, self.start : self.start + self.count]
        ids = ids.astype(jnp.float32).astype(jnp.int32)[:1]
        clusters = lax.broadcasted_iota(jnp.int32, (CL_DEV, self.count), 0)
        return (clusters + 1 == ids).astype(jnp.bfloat16)


def stack_kernel(*refs):
    *in_refs, out_ref = refs
    place = 0
    for in_ref in in_refs:
        out_ref[place : place + in_ref.shape[0], :] = in_ref[...]
        place += in_ref.shape[0]


def stack(*arrays, after=(), cost=None):
    rows = sum(one.shape[0] for one in arrays)
    return call(stack_kernel, [bf16(rows, arrays[0].shape[1])], arrays, after=after, cost=cost)[0]


def kern(rows, slots, slot_norms):
    inner = dot(rows, slots, NT)
    squared = column_norms(rows) + slot_norms - 2.0 * inner
    return jnp.exp(squared * (-1.0 / rows.shape[1])).astype(jnp.bfloat16)


def row_norms(slots_ref):
    pieces = [
        row_of(column_norms(slots_ref[start : start + CL_DEV, :]))
        for start in range(0, slots_ref.shape[0], CL_DEV)
    ]
    return jnp.concatenate(pieces, axis=1)


def chunks(begin, end, step):
    return [(start, min(start + step, end)) for start in range(begin, end, step)]


def sums_kernel(counts, parts, *refs):
    *array_refs, left_ref, hot_ref, sums_ref, totals_ref = refs
    rows, (total, width) = sums_ref.shape[0], left_ref.shape
    place = 0
    for array_ref, count in zip(array_refs, counts):
        for t in range(width // LANES):
            left_ref[place : place + count, t * LANES : (t + 1) * LANES] = array_ref[
                t * count : (t + 1) * count, :
            ]
        place += count
    for n, *rest in parts:
        part = Half(array_refs[n], *rest)
        end = place + part.count
        part.put(left_ref, place)
        hot_ref[:, place - rows : end - rows] = part.indicator(width)
        place = end
    slots, hot = left_ref[rows:, :], hot_ref[...]
    norms = row_norms(left_ref.at[rows:])
    for start, end in chunks(0, rows, 256):
        sums_ref[start:end, :] = dot(kern(left_ref[start:end, :], slots, norms), hot, NT)
    shares = jnp.zeros(hot.shape, jnp.float32)
    for start, end in chunks(rows, total, 256):
        tile = kern(left_ref[start:end, :], slots, norms)
        shares += dot(hot_ref[:, start - rows : end - rows], tile, NN)
    column = jnp.sum(shares * hot.astype(jnp.float32), axis=1, keepdims=True)
    ones = jnp.ones((8, total - rows), jnp.bfloat16)
    totals_ref[:8, :] = jnp.broadcast_to(row_of(column), (8, CL_DEV))
    totals_ref[8:, :] = dot(ones, hot, NT)


def distance_kernel(parts, order, *refs):
    left_ref, old_hot_ref, sums_ref, totals_ref, *refs = refs
    *array_refs, out_ref, slots_ref, hot_ref = refs
    rows, total = sums_ref.shape[0], left_ref.shape[0]
    place = 0
    for n, *rest in parts:
        part = Half(array_refs[n], *rest)
        end = place + part.count
        part.put(slots_ref, place)
        hot_ref[:, place:end] = part.indicator(slots_ref.shape[1])
        place = end
    slots, hot = slots_ref[...], hot_ref[...]
    norms = row_norms(slots_ref)
    shares = dot(hot, kern(slots, slots, norms), NN)
    for start, end in chunks(rows, total, 512):
        tile = kern(left_ref[start:end, :], slots, norms)
        shares += 2.0 * dot(old_hot_ref[:, start - rows : end - rows], tile, NN)
    column = jnp.sum(shares * hot.astype(jnp.float32), axis=1, keepdims=True)
    totals = totals_ref[:1, :] + row_of(column)
    counts = totals_ref[8:9, :] + dot(jnp.ones((8, place), jnp.bfloat16), hot, NT)[:1]
    sizes = jnp.maximum(counts, 1.0)
    offset = 1.0 + totals / (sizes * sizes)
    factor = 2.0 / sizes
    me = lax.axis_index("col")
    own_count = rows // len(order)
    for start, end in chunks(0, rows, 512):
        part = sums_ref[start:end, :] + dot(kern(left_ref[start:end, :], slots, norms), hot, NT)
        part = offset - part * factor
        for b in range((end - start) // own_count):
            row = pl.multiple_of((me ^ order[start // own_count + b]) * own_count, own_count)
            out_ref[pl.ds(row, own_count), :] = part[b * own_count : (b + 1) * own_count]


def parts_of(sets, arrays, width):
    parts = []
    for one, base, count, second in sets:
        n = [array is one for array in arrays].index(True)
        for start in range(base, one.shape[0], 2 * count * width // LANES + ID_ROWS):
            parts.append((n, start, count, second))
    return parts


def cost_of(rows, slots, width):
    return pl.CostEstimate(
        flops=2 * rows * slots * (width + CL_DEV),
        bytes_accessed=2 * rows * width,
        transcendentals=rows * slots,
    )


def sum_slots(local, sets, width):
    arrays = [one for one, _ in local] + [one for one, base, *_ in sets if not base]
    counts = [base * LANES // width for _, base in local]
    parts = parts_of(sets, arrays, width)
    rows, slots = sum(counts), sum(part[2] for part in parts)
    return call(
        functools.partial(sums_kernel, counts, parts),
        [
            bf16(rows + slots, width),
            bf16(CL_DEV, slots),
            jax.ShapeDtypeStruct((rows, CL_DEV), jnp.float32),
            jax.ShapeDtypeStruct((16, CL_DEV), jnp.float32),
        ],
        arrays,
        mib=32,
        cost=cost_of(1 * (rows + slots), slots, width),
    )


def finish(order, sums, sets, width):
    arrays = [one for one, *_ in sets]
    parts = parts_of(sets, arrays, width)
    slots = sum(part[2] for part in parts)
    return call(
        functools.partial(distance_kernel, parts, order),
        [jax.ShapeDtypeStruct(sums[2].shape, jnp.float32)],
        [*sums, *arrays],
        [pltpu.VMEM((slots, width), jnp.bfloat16), pltpu.VMEM((CL_DEV, slots), jnp.bfloat16)],
        mib=32,
        cost=cost_of(sums[0].shape[0] + slots, slots, width),
    )[0]


def per_device(points, assign):
    own_count, width = points.shape
    group_count, row_count = lax.axis_size("col"), lax.axis_size("row")
    chips, tiles = group_count // 2, width // LANES
    slots = max(2, 2 * own_count // group_count)

    def over_col(values, bits):
        return lax.ppermute(values, "col", [(i, i ^ bits) for i in range(group_count)])

    def over_row(values, bits):
        return lax.ppermute(values, "row", [(i, i ^ bits) for i in range(row_count)])

    def pending(one, flops):
        return stack(one, cost=pl.CostEstimate(flops=int(flops), bytes_accessed=0, transcendentals=0))

    def label(values, ids):
        return call(label_kernel, [bf16(own_count * tiles + ID_ROWS, LANES)], [values, ids])[0]

    assign = assign.reshape(1, own_count)
    far = chips // 2
    blocks = {0: label(points, assign)}
    for q in sorted({far, 1}, reverse=True):
        blocks[q] = label(pending(over_col(points, 2 * q), 1e8 if q > 1 else 4e9), over_col(assign, 2 * q))
    bit = far // 2
    while bit:
        for q in range(0, chips, 2 * bit):
            if q + bit not in blocks:
                blocks[q + bit] = pending(over_col(blocks[q], 2 * bit), 1e9)
        bit //= 2
    places, near, last = [], [], []
    for batch in (range(2), range(2, chips)):
        base, half = len(batch) * own_count * tiles, len(batch) * slots
        set_rows = 2 * half * tiles + ID_ROWS
        here, sets = call(
            functools.partial(select_kernel, slots),
            [bf16(base + set_rows, LANES), bf16(set_rows, LANES)],
            [blocks[q] for q in batch],
            [pltpu.VMEM((len(batch) * own_count, width), jnp.bfloat16)],
            after=[] if last else [blocks[far]],
        )
        got = [over_row(sets, bits) for bits in range(row_count - 1, 0, -1)]
        places.append([2 * q for q in batch])
        near.append((here, base, half))
        last.append((got, 0, half))

    def both_cores(one, base, half):
        return [(one, base, half, False), (over_col(one, 1), base, half, True)]

    pairs = [both_cores(*one) for one in near]
    local = [pair[side][:2] for side in range(2) for pair in pairs]
    got, base, half = last[0]
    old = [*pairs[0], *both_cores(stack(*got), base, half)]
    order = [q for side in range(2) for batch in places for q in (one ^ side for one in batch)]
    sums = sum_slots(local, old, width)
    got, base, half = last[1]
    return finish(order, sums, [*pairs[1], *both_cores(stack(*got), base, half)], width)


def solution(mesh):
    return jax.shard_map(
        per_device,
        mesh=mesh,
        in_specs=(P(("row", "col"), None), P(("row", "col"))),
        out_specs=P("row", "col"),
        check_vma=False,
    )
```

```python
import functools

import jax
import jax.numpy as jnp
from jax import lax
from jax.experimental import pallas as pl
from jax.experimental.pallas import tpu as pltpu
from jax.sharding import PartitionSpec as P

CL_DEV = 128
ID_ROWS = 8
LANES = 128
NT = (((1,), (1,)), ((), ()))
NN = (((1,), (0,)), ((), ()))
VMEM = pl.BlockSpec(memory_space=pltpu.VMEM)
MIB = 1024 * 1024


def dot(left, right, dims):
    return lax.dot_general(left, right, dims, preferred_element_type=jnp.float32)


def bf16(*shape):
    return jax.ShapeDtypeStruct(shape, jnp.bfloat16)


def call(kernel, out_shape, args, scratch=(), mib=8, after=(), cost=None):
    count = len(args)

    def body(*refs):
        kernel(*refs[:count], *refs[count + len(after) :])

    return pl.pallas_call(
        body,
        out_shape=out_shape,
        in_specs=[VMEM] * count + [pl.BlockSpec(memory_space=pl.ANY)] * len(after),
        out_specs=[VMEM] * len(out_shape),
        scratch_shapes=scratch,
        compiler_params=pltpu.CompilerParams(vmem_limit_bytes=mib * MIB),
        cost_estimate=cost,
    )(*args, *after)


def tall(rows):
    return [rows[:, start : start + LANES] for start in range(0, rows.shape[1], LANES)]


def put_tall(ref, base, rows):
    count = rows.shape[0]
    for t, piece in enumerate(tall(rows)):
        ref[base + t * count : base + (t + 1) * count, :] = piece


def label_kernel(points_ref, assign_ref, out_ref):
    own_count = points_ref.shape[0]
    assign = assign_ref[...]
    group_of = assign // CL_DEV
    put_tall(out_ref, 0, points_ref[...])
    end = out_ref.shape[0] - ID_ROWS
    out_ref[end:, :] = jnp.zeros((ID_ROWS, LANES), jnp.bfloat16)
    for n, labels in enumerate((group_of, assign - group_of * CL_DEV)):
        out_ref[end:, n * own_count : (n + 1) * own_count] = jnp.broadcast_to(
            labels.astype(jnp.float32), (ID_ROWS, own_count)
        ).astype(jnp.bfloat16)


def select_kernel(slots, *refs):
    *block_refs, local_ref, set_ref, points_ref = refs
    count = len(block_refs)
    points, width = points_ref.shape
    own_count = points // count
    half = count * slots
    me = lax.axis_index("col")
    earlier = (
        lax.broadcasted_iota(jnp.int32, (own_count, own_count), 0)
        < lax.broadcasted_iota(jnp.int32, (own_count, own_count), 1)
    ).astype(jnp.bfloat16)
    slot = lax.broadcasted_iota(jnp.int32, (2 * half, own_count), 0)
    relatives, labels = [], []
    for n, block_ref in enumerate(block_refs):
        for t in range(width // LANES):
            points_ref[n * own_count : (n + 1) * own_count, t * LANES : (t + 1) * LANES] = block_ref[
                t * own_count : (t + 1) * own_count, :
            ]
        end = block_ref.shape[0] - ID_ROWS
        group_of = block_ref[end:, :own_count].astype(jnp.float32).astype(jnp.int32)
        relatives.append(group_of ^ me)
        labels.append(block_ref[end:, own_count : 2 * own_count].astype(jnp.float32) + 1.0)
    members = [
        lax.broadcasted_iota(jnp.int32, (ID_ROWS, own_count), 0) == relative
        for relative in relatives
    ]
    marks = [member.astype(jnp.float32) for member in members]
    ranks = dot(jnp.concatenate(marks, axis=0).astype(jnp.bfloat16), earlier, NN)
    dispatch = []
    for n, (relative, mark) in enumerate(zip(relatives, marks)):
        rank = ranks[n * ID_ROWS : (n + 1) * ID_ROWS] * mark
        position = jnp.sum(rank, axis=0, keepdims=True).astype(jnp.int32)
        target = jnp.where(relative < 2, relative * half + n * slots + position, -1)
        dispatch.append((slot == target[:1]).astype(jnp.bfloat16))
    dispatch = jnp.concatenate(dispatch, axis=1)
    rows = dot(dispatch, points_ref[...], NN).astype(jnp.bfloat16)
    ids = dot(jnp.concatenate(labels, axis=1).astype(jnp.bfloat16), dispatch, NT)
    put_tall(local_ref, 0, points_ref[...])
    for ref, start in ((local_ref, points * width // LANES), (set_ref, 0)):
        end = ref.shape[0] - ID_ROWS
        put_tall(ref, start, rows)
        ref[end:, :] = jnp.zeros((ID_ROWS, LANES), jnp.bfloat16)
        ref[end:, : 2 * half] = ids.astype(jnp.bfloat16)


def column_norms(rows):
    values = rows.astype(jnp.float32)
    return jnp.sum(values * values, axis=1, keepdims=True)


def row_of(column):
    return jnp.transpose(jnp.broadcast_to(column, (column.shape[0], 128)))[:1]


class Half:
    def __init__(self, ref, base, count, second):
        self.ref, self.base, self.count = ref, base, count
        self.start = count if second else 0

    def put(self, out_ref, place):
        for t in range(out_ref.shape[1] // LANES):
            start = self.base + 2 * t * self.count + self.start
            out_ref[place : place + self.count, t * LANES : (t + 1) * LANES] = self.ref[
                start : start + self.count, :
            ]

    def indicator(self, width):
        base = self.base + 2 * self.count * width // LANES
        ids = self.ref[base : base + ID_ROWS, self.start : self.start + self.count]
        ids = ids.astype(jnp.float32).astype(jnp.int32)[:1]
        clusters = lax.broadcasted_iota(jnp.int32, (CL_DEV, self.count), 0)
        return (clusters + 1 == ids).astype(jnp.bfloat16)


def stack_kernel(*refs):
    *in_refs, out_ref = refs
    place = 0
    for in_ref in in_refs:
        out_ref[place : place + in_ref.shape[0], :] = in_ref[...]
        place += in_ref.shape[0]


def stack(*arrays, after=(), cost=None):
    rows = sum(one.shape[0] for one in arrays)
    return call(stack_kernel, [bf16(rows, arrays[0].shape[1])], arrays, after=after, cost=cost)[0]


def kern(rows, slots, slot_norms):
    inner = dot(rows, slots, NT)
    squared = column_norms(rows) + slot_norms - 2.0 * inner
    return jnp.exp(squared * (-1.0 / rows.shape[1])).astype(jnp.bfloat16)


def row_norms(slots_ref):
    pieces = [
        row_of(column_norms(slots_ref[start : start + CL_DEV, :]))
        for start in range(0, slots_ref.shape[0], CL_DEV)
    ]
    return jnp.concatenate(pieces, axis=1)


def chunks(begin, end, step):
    return [(start, min(start + step, end)) for start in range(begin, end, step)]


def sums_kernel(counts, parts, *refs):
    *array_refs, left_ref, hot_ref, sums_ref, totals_ref = refs
    rows, (total, width) = sums_ref.shape[0], left_ref.shape
    place = 0
    for array_ref, count in zip(array_refs, counts):
        for t in range(width // LANES):
            left_ref[place : place + count, t * LANES : (t + 1) * LANES] = array_ref[
                t * count : (t + 1) * count, :
            ]
        place += count
    for n, *rest in parts:
        part = Half(array_refs[n], *rest)
        end = place + part.count
        part.put(left_ref, place)
        hot_ref[:, place - rows : end - rows] = part.indicator(width)
        place = end
    slots, hot = left_ref[rows:, :], hot_ref[...]
    norms = row_norms(left_ref.at[rows:])
    for start, end in chunks(0, rows, 256):
        sums_ref[start:end, :] = dot(kern(left_ref[start:end, :], slots, norms), hot, NT)
    shares = jnp.zeros(hot.shape, jnp.float32)
    for start, end in chunks(rows, total, 256):
        tile = kern(left_ref[start:end, :], slots, norms)
        shares += dot(hot_ref[:, start - rows : end - rows], tile, NN)
    column = jnp.sum(shares * hot.astype(jnp.float32), axis=1, keepdims=True)
    ones = jnp.ones((8, total - rows), jnp.bfloat16)
    totals_ref[:8, :] = jnp.broadcast_to(row_of(column), (8, CL_DEV))
    totals_ref[8:, :] = dot(ones, hot, NT)


def distance_kernel(parts, order, *refs):
    left_ref, old_hot_ref, sums_ref, totals_ref, *refs = refs
    *array_refs, out_ref, slots_ref, hot_ref = refs
    rows, total = sums_ref.shape[0], left_ref.shape[0]
    place = 0
    for n, *rest in parts:
        part = Half(array_refs[n], *rest)
        end = place + part.count
        part.put(slots_ref, place)
        hot_ref[:, place:end] = part.indicator(slots_ref.shape[1])
        place = end
    slots, hot = slots_ref[...], hot_ref[...]
    norms = row_norms(slots_ref)
    whole = kern(left_ref[...], slots, norms) if total * place <= MIB else None

    def tiles(begin, end):
        if whole is not None:
            yield begin, end, whole[begin:end]
            return
        for start, stop in chunks(begin, end, 512):
            yield start, stop, kern(left_ref[start:stop, :], slots, norms)

    shares = dot(hot, kern(slots, slots, norms), NN)
    for start, end, tile in tiles(rows, total):
        shares += 2.0 * dot(old_hot_ref[:, start - rows : end - rows], tile, NN)
    column = jnp.sum(shares * hot.astype(jnp.float32), axis=1, keepdims=True)
    totals = totals_ref[:1, :] + row_of(column)
    counts = totals_ref[8:9, :] + dot(jnp.ones((8, place), jnp.bfloat16), hot, NT)[:1]
    sizes = jnp.maximum(counts, 1.0)
    offset = 1.0 + totals / (sizes * sizes)
    factor = 2.0 / sizes
    me = lax.axis_index("col")
    own_count = rows // len(order)
    for start, end, tile in tiles(0, rows):
        part = offset - (sums_ref[start:end, :] + dot(tile, hot, NT)) * factor
        for b in range((end - start) // own_count):
            row = pl.multiple_of((me ^ order[start // own_count + b]) * own_count, own_count)
            out_ref[pl.ds(row, own_count), :] = part[b * own_count : (b + 1) * own_count]


def parts_of(sets, arrays, width):
    parts = []
    for one, base, count, second in sets:
        n = [array is one for array in arrays].index(True)
        for start in range(base, one.shape[0], 2 * count * width // LANES + ID_ROWS):
            parts.append((n, start, count, second))
    return parts


def cost_of(rows, slots, width):
    return pl.CostEstimate(
        flops=2 * rows * slots * (width + CL_DEV),
        bytes_accessed=2 * rows * width,
        transcendentals=rows * slots,
    )


def sum_slots(local, sets, width):
    arrays = [one for one, _ in local] + [one for one, base, *_ in sets if not base]
    counts = [base * LANES // width for _, base in local]
    parts = parts_of(sets, arrays, width)
    rows, slots = sum(counts), sum(part[2] for part in parts)
    return call(
        functools.partial(sums_kernel, counts, parts),
        [
            bf16(rows + slots, width),
            bf16(CL_DEV, slots),
            jax.ShapeDtypeStruct((rows, CL_DEV), jnp.float32),
            jax.ShapeDtypeStruct((16, CL_DEV), jnp.float32),
        ],
        arrays,
        mib=32,
        cost=cost_of(1 * (rows + slots), slots, width),
    )


def finish(order, sums, sets, width):
    arrays = [one for one, *_ in sets]
    parts = parts_of(sets, arrays, width)
    slots = sum(part[2] for part in parts)
    return call(
        functools.partial(distance_kernel, parts, order),
        [jax.ShapeDtypeStruct(sums[2].shape, jnp.float32)],
        [*sums, *arrays],
        [pltpu.VMEM((slots, width), jnp.bfloat16), pltpu.VMEM((CL_DEV, slots), jnp.bfloat16)],
        mib=32,
        cost=cost_of(sums[0].shape[0] + slots, slots, width),
    )[0]


def per_device(points, assign):
    own_count, width = points.shape
    group_count, row_count = lax.axis_size("col"), lax.axis_size("row")
    chips, tiles = group_count // 2, width // LANES
    slots = max(2, 2 * own_count // group_count)

    def over_col(values, bits):
        return lax.ppermute(values, "col", [(i, i ^ bits) for i in range(group_count)])

    def over_row(values, bits):
        return lax.ppermute(values, "row", [(i, i ^ bits) for i in range(row_count)])

    def pending(one, flops):
        return stack(one, cost=pl.CostEstimate(flops=int(flops), bytes_accessed=0, transcendentals=0))

    def label(values, ids):
        return call(label_kernel, [bf16(own_count * tiles + ID_ROWS, LANES)], [values, ids])[0]

    assign = assign.reshape(1, own_count)
    far = chips // 2
    blocks = {0: label(points, assign)}
    for q in sorted({far, 1}, reverse=True):
        blocks[q] = label(pending(over_col(points, 2 * q), 1e8 if q > 1 else 4e9), over_col(assign, 2 * q))
    bit = far // 2
    while bit:
        for q in range(0, chips, 2 * bit):
            if q + bit not in blocks:
                blocks[q + bit] = pending(over_col(blocks[q], 2 * bit), 1e9)
        bit //= 2
    places, near, last = [], [], []
    for batch in (range(2), range(2, chips)):
        base, half = len(batch) * own_count * tiles, len(batch) * slots
        set_rows = 2 * half * tiles + ID_ROWS
        here, sets = call(
            functools.partial(select_kernel, slots),
            [bf16(base + set_rows, LANES), bf16(set_rows, LANES)],
            [blocks[q] for q in batch],
            [pltpu.VMEM((len(batch) * own_count, width), jnp.bfloat16)],
            after=[] if last else [blocks[far]],
        )
        got = [over_row(sets, bits) for bits in range(row_count - 1, 0, -1)]
        places.append([2 * q for q in batch])
        near.append((here, base, half))
        last.append((got, 0, half))

    def both_cores(one, base, half):
        return [(one, base, half, False), (over_col(one, 1), base, half, True)]

    pairs = [both_cores(*one) for one in near]
    local = [pair[side][:2] for side in range(2) for pair in pairs]
    got, base, half = last[0]
    old = [*pairs[0], *both_cores(stack(*got), base, half)]
    order = [q for side in range(2) for batch in places for q in (one ^ side for one in batch)]
    sums = sum_slots(local, old, width)
    got, base, half = last[1]
    return finish(order, sums, [*pairs[1], *both_cores(stack(*got), base, half)], width)


def solution(mesh):
    return jax.shard_map(
        per_device,
        mesh=mesh,
        in_specs=(P(("row", "col"), None), P(("row", "col"))),
        out_specs=P("row", "col"),
        check_vma=False,
    )
```

```python
import functools

import jax
import jax.numpy as jnp
from jax import lax
from jax.experimental import pallas as pl
from jax.experimental.pallas import tpu as pltpu
from jax.sharding import PartitionSpec as P

CL_DEV = 128
ID_ROWS = 8
LANES = 128
NT = (((1,), (1,)), ((), ()))
NN = (((1,), (0,)), ((), ()))
VMEM = pl.BlockSpec(memory_space=pltpu.VMEM)
MIB = 1024 * 1024


def dot(left, right, dims):
    return lax.dot_general(left, right, dims, preferred_element_type=jnp.float32)


def bf16(*shape):
    return jax.ShapeDtypeStruct(shape, jnp.bfloat16)


def call(kernel, out_shape, args, scratch=(), mib=8, after=(), cost=None):
    count = len(args)

    def body(*refs):
        kernel(*refs[:count], *refs[count + len(after) :])

    return pl.pallas_call(
        body,
        out_shape=out_shape,
        in_specs=[VMEM] * count + [pl.BlockSpec(memory_space=pl.ANY)] * len(after),
        out_specs=[VMEM] * len(out_shape),
        scratch_shapes=scratch,
        compiler_params=pltpu.CompilerParams(vmem_limit_bytes=mib * MIB),
        cost_estimate=cost,
    )(*args, *after)


def tall(rows):
    return [rows[:, start : start + LANES] for start in range(0, rows.shape[1], LANES)]


def put_tall(ref, base, rows):
    count = rows.shape[0]
    for t, piece in enumerate(tall(rows)):
        ref[base + t * count : base + (t + 1) * count, :] = piece


def label_kernel(points_ref, assign_ref, out_ref):
    own_count = points_ref.shape[0]
    assign = assign_ref[...]
    group_of = assign // CL_DEV
    put_tall(out_ref, 0, points_ref[...])
    end = out_ref.shape[0] - ID_ROWS
    out_ref[end:, :] = jnp.zeros((ID_ROWS, LANES), jnp.bfloat16)
    for n, labels in enumerate((group_of, assign - group_of * CL_DEV)):
        out_ref[end:, n * own_count : (n + 1) * own_count] = jnp.broadcast_to(
            labels.astype(jnp.float32), (ID_ROWS, own_count)
        ).astype(jnp.bfloat16)


def select_kernel(slots, *refs):
    *block_refs, local_ref, set_ref, points_ref = refs
    count = len(block_refs)
    points, width = points_ref.shape
    own_count = points // count
    half = count * slots
    me = lax.axis_index("col")
    earlier = (
        lax.broadcasted_iota(jnp.int32, (own_count, own_count), 0)
        < lax.broadcasted_iota(jnp.int32, (own_count, own_count), 1)
    ).astype(jnp.bfloat16)
    slot = lax.broadcasted_iota(jnp.int32, (2 * half, own_count), 0)
    relatives, labels = [], []
    for n, block_ref in enumerate(block_refs):
        for t in range(width // LANES):
            points_ref[n * own_count : (n + 1) * own_count, t * LANES : (t + 1) * LANES] = block_ref[
                t * own_count : (t + 1) * own_count, :
            ]
        end = block_ref.shape[0] - ID_ROWS
        group_of = block_ref[end:, :own_count].astype(jnp.float32).astype(jnp.int32)
        relatives.append(group_of ^ me)
        labels.append(block_ref[end:, own_count : 2 * own_count].astype(jnp.float32) + 1.0)
    members = [
        lax.broadcasted_iota(jnp.int32, (ID_ROWS, own_count), 0) == relative
        for relative in relatives
    ]
    marks = [member.astype(jnp.float32) for member in members]
    ranks = dot(jnp.concatenate(marks, axis=0).astype(jnp.bfloat16), earlier, NN)
    dispatch = []
    for n, (relative, mark) in enumerate(zip(relatives, marks)):
        rank = ranks[n * ID_ROWS : (n + 1) * ID_ROWS] * mark
        position = jnp.sum(rank, axis=0, keepdims=True).astype(jnp.int32)
        target = jnp.where(relative < 2, relative * half + n * slots + position, -1)
        dispatch.append((slot == target[:1]).astype(jnp.bfloat16))
    dispatch = jnp.concatenate(dispatch, axis=1)
    rows = dot(dispatch, points_ref[...], NN).astype(jnp.bfloat16)
    ids = dot(jnp.concatenate(labels, axis=1).astype(jnp.bfloat16), dispatch, NT)
    put_tall(local_ref, 0, points_ref[...])
    for ref, start in ((local_ref, points * width // LANES), (set_ref, 0)):
        end = ref.shape[0] - ID_ROWS
        put_tall(ref, start, rows)
        ref[end:, :] = jnp.zeros((ID_ROWS, LANES), jnp.bfloat16)
        ref[end:, : 2 * half] = ids.astype(jnp.bfloat16)


def column_norms(rows):
    values = rows.astype(jnp.float32)
    return jnp.sum(values * values, axis=1, keepdims=True)


def row_of(column):
    return jnp.transpose(jnp.broadcast_to(column, (column.shape[0], 128)))[:1]


class Half:
    def __init__(self, ref, base, count, second):
        self.ref, self.base, self.count = ref, base, count
        self.start = count if second else 0

    def put(self, out_ref, place):
        for t in range(out_ref.shape[1] // LANES):
            start = self.base + 2 * t * self.count + self.start
            out_ref[place : place + self.count, t * LANES : (t + 1) * LANES] = self.ref[
                start : start + self.count, :
            ]

    def indicator(self, width):
        base = self.base + 2 * self.count * width // LANES
        ids = self.ref[base : base + ID_ROWS, self.start : self.start + self.count]
        ids = ids.astype(jnp.float32).astype(jnp.int32)[:1]
        clusters = lax.broadcasted_iota(jnp.int32, (CL_DEV, self.count), 0)
        return (clusters + 1 == ids).astype(jnp.bfloat16)


def aligned(rows):
    return -(-rows // 16) * 16


def stack_kernel(*refs):
    *in_refs, out_ref = refs
    place = 0
    for in_ref in in_refs:
        out_ref[place : place + in_ref.shape[0], :] = in_ref[...]
        place += aligned(in_ref.shape[0])


def stack(*arrays, cost=None):
    rows = sum(aligned(one.shape[0]) for one in arrays[:-1]) + arrays[-1].shape[0]
    shape = jax.ShapeDtypeStruct((rows, arrays[0].shape[1]), arrays[0].dtype)
    return call(stack_kernel, [shape], arrays, cost=cost)[0]


def kern(rows, slots, slot_norms):
    inner = dot(rows, slots, NT)
    squared = column_norms(rows) + slot_norms - 2.0 * inner
    return jnp.exp(squared * (-1.0 / rows.shape[1])).astype(jnp.bfloat16)


def row_norms(slots_ref):
    pieces = [
        row_of(column_norms(slots_ref[start : start + CL_DEV, :]))
        for start in range(0, slots_ref.shape[0], CL_DEV)
    ]
    return jnp.concatenate(pieces, axis=1)


def chunks(begin, end, step):
    return [(start, min(start + step, end)) for start in range(begin, end, step)]


def sums_kernel(counts, parts, *refs):
    *array_refs, left_ref, hot_ref, sums_ref, totals_ref = refs
    rows, (total, width) = sums_ref.shape[0], left_ref.shape
    place = 0
    for array_ref, count in zip(array_refs, counts):
        for t in range(width // LANES):
            left_ref[place : place + count, t * LANES : (t + 1) * LANES] = array_ref[
                t * count : (t + 1) * count, :
            ]
        place += count
    for n, *rest in parts:
        part = Half(array_refs[n], *rest)
        end = place + part.count
        part.put(left_ref, place)
        hot_ref[:, place - rows : end - rows] = part.indicator(width)
        place = end
    slots, hot = left_ref[rows:, :], hot_ref[...]
    norms = row_norms(left_ref.at[rows:])
    for start, end in chunks(0, rows, 256):
        sums_ref[start:end, :] = dot(kern(left_ref[start:end, :], slots, norms), hot, NT)
    shares = jnp.zeros(hot.shape, jnp.float32)
    for start, end in chunks(rows, total, 256):
        tile = kern(left_ref[start:end, :], slots, norms)
        shares += dot(hot_ref[:, start - rows : end - rows], tile, NN)
    column = jnp.sum(shares * hot.astype(jnp.float32), axis=1, keepdims=True)
    ones = jnp.ones((8, total - rows), jnp.bfloat16)
    totals_ref[:8, :] = jnp.broadcast_to(row_of(column), (8, CL_DEV))
    totals_ref[8:, :] = dot(ones, hot, NT)


def distance_kernel(parts, order, *refs):
    left_ref, old_hot_ref, sums_ref, totals_ref, *refs = refs
    *array_refs, out_ref, slots_ref, hot_ref = refs
    rows, total = sums_ref.shape[0], left_ref.shape[0]
    place = 0
    for n, *rest in parts:
        part = Half(array_refs[n], *rest)
        end = place + part.count
        part.put(slots_ref, place)
        hot_ref[:, place:end] = part.indicator(slots_ref.shape[1])
        place = end
    slots, hot = slots_ref[...], hot_ref[...]
    norms = row_norms(slots_ref)
    whole = kern(left_ref[...], slots, norms) if total * place <= MIB else None

    def tiles(begin, end):
        if whole is not None:
            yield begin, end, whole[begin:end]
            return
        for start, stop in chunks(begin, end, 512):
            yield start, stop, kern(left_ref[start:stop, :], slots, norms)

    shares = dot(hot, kern(slots, slots, norms), NN)
    for start, end, tile in tiles(rows, total):
        shares += 2.0 * dot(old_hot_ref[:, start - rows : end - rows], tile, NN)
    column = jnp.sum(shares * hot.astype(jnp.float32), axis=1, keepdims=True)
    totals = totals_ref[:1, :] + row_of(column)
    counts = totals_ref[8:9, :] + dot(jnp.ones((8, place), jnp.bfloat16), hot, NT)[:1]
    sizes = jnp.maximum(counts, 1.0)
    offset = 1.0 + totals / (sizes * sizes)
    factor = 2.0 / sizes
    me = lax.axis_index("col")
    own_count = rows // len(order)
    for start, end, tile in tiles(0, rows):
        part = offset - (sums_ref[start:end, :] + dot(tile, hot, NT)) * factor
        for b in range((end - start) // own_count):
            row = pl.multiple_of((me ^ order[start // own_count + b]) * own_count, own_count)
            out_ref[pl.ds(row, own_count), :] = part[b * own_count : (b + 1) * own_count]


def parts_of(sets, arrays, width):
    parts = []
    for one, base, count, second in sets:
        n = [array is one for array in arrays].index(True)
        for start in range(base, one.shape[0], aligned(2 * count * width // LANES + ID_ROWS)):
            parts.append((n, start, count, second))
    return parts


def cost_of(rows, slots, width):
    return pl.CostEstimate(
        flops=2 * rows * slots * (width + CL_DEV),
        bytes_accessed=2 * rows * width,
        transcendentals=rows * slots,
    )


def sum_slots(local, sets, width):
    arrays = [one for one, _ in local] + [one for one, base, *_ in sets if not base]
    counts = [base * LANES // width for _, base in local]
    parts = parts_of(sets, arrays, width)
    rows, slots = sum(counts), sum(part[2] for part in parts)
    return call(
        functools.partial(sums_kernel, counts, parts),
        [
            bf16(rows + slots, width),
            bf16(CL_DEV, slots),
            jax.ShapeDtypeStruct((rows, CL_DEV), jnp.float32),
            jax.ShapeDtypeStruct((16, CL_DEV), jnp.float32),
        ],
        arrays,
        mib=32,
        cost=cost_of(1 * (rows + slots), slots, width),
    )


def finish(order, sums, sets, width):
    arrays = [one for one, *_ in sets]
    parts = parts_of(sets, arrays, width)
    slots = sum(part[2] for part in parts)
    return call(
        functools.partial(distance_kernel, parts, order),
        [jax.ShapeDtypeStruct(sums[2].shape, jnp.float32)],
        [*sums, *arrays],
        [pltpu.VMEM((slots, width), jnp.bfloat16), pltpu.VMEM((CL_DEV, slots), jnp.bfloat16)],
        mib=32,
        cost=cost_of(sums[0].shape[0] + slots, slots, width),
    )[0]


def per_device(points, assign):
    own_count, width = points.shape
    group_count, row_count = lax.axis_size("col"), lax.axis_size("row")
    chips, tiles = group_count // 2, width // LANES
    slots = max(2, 2 * own_count // group_count)

    def over_col(values, bits):
        return lax.ppermute(values, "col", [(i, i ^ bits) for i in range(group_count)])

    def over_row(values, bits):
        return lax.ppermute(values, "row", [(i, i ^ bits) for i in range(row_count)])

    def pending(one, flops):
        return stack(one, cost=pl.CostEstimate(flops=int(flops), bytes_accessed=0, transcendentals=0))

    def label(values, ids):
        return call(label_kernel, [bf16(own_count * tiles + ID_ROWS, LANES)], [values, ids])[0]

    assign = assign.reshape(1, own_count)
    far = chips // 2
    blocks = {0: label(points, assign)}
    for q in sorted({far, 1}, reverse=True):
        blocks[q] = label(pending(over_col(points, 2 * q), 1e8 if q > 1 else 4e9), over_col(assign, 2 * q))
    bit = far // 2
    while bit:
        for q in range(0, chips, 2 * bit):
            if q + bit not in blocks:
                blocks[q + bit] = pending(over_col(blocks[q], 2 * bit), 1e9)
        bit //= 2
    places, near, last = [], [], []
    for batch in (range(2), range(2, chips)):
        base, half = len(batch) * own_count * tiles, len(batch) * slots
        set_rows = 2 * half * tiles + ID_ROWS
        here, sets = call(
            functools.partial(select_kernel, slots),
            [bf16(base + set_rows, LANES), bf16(set_rows, LANES)],
            [blocks[q] for q in batch],
            [pltpu.VMEM((len(batch) * own_count, width), jnp.bfloat16)],
            after=[] if last else [blocks[far]],
        )
        got = [over_row(sets, bits) for bits in range(row_count - 1, 0, -1)]
        places.append([2 * q for q in batch])
        near.append((here, base, half))
        last.append((got, 0, half))

    def both_cores(one, base, half):
        return [(one, base, half, False), (over_col(one, 1), base, half, True)]

    pairs = [both_cores(*one) for one in near]
    local = [pair[side][:2] for side in range(2) for pair in pairs]
    got, base, half = last[0]
    old = [*pairs[0], *both_cores(stack(*got), base, half)]
    order = [q for side in range(2) for batch in places for q in (one ^ side for one in batch)]
    sums = sum_slots(local, old, width)
    got, base, half = last[1]
    return finish(order, sums, [*pairs[1], *both_cores(stack(*got), base, half)], width)


def solution(mesh):
    return jax.shard_map(
        per_device,
        mesh=mesh,
        in_specs=(P(("row", "col"), None), P(("row", "col"))),
        out_specs=P("row", "col"),
        check_vma=False,
    )
```

```python
import functools

import jax
import jax.numpy as jnp
from jax import lax
from jax.experimental import pallas as pl
from jax.experimental.pallas import tpu as pltpu
from jax.sharding import PartitionSpec as P

CL_DEV = 128
ID_ROWS = 8
LANES = 128
NT = (((1,), (1,)), ((), ()))
NN = (((1,), (0,)), ((), ()))
VMEM = pl.BlockSpec(memory_space=pltpu.VMEM)
MIB = 1024 * 1024


def dot(left, right, dims):
    return lax.dot_general(left, right, dims, preferred_element_type=jnp.float32)


def bf16(*shape):
    return jax.ShapeDtypeStruct(shape, jnp.bfloat16)


def call(kernel, out_shape, args, scratch=(), mib=8, after=(), cost=None):
    count = len(args)

    def body(*refs):
        kernel(*refs[:count], *refs[count + len(after) :])

    return pl.pallas_call(
        body,
        out_shape=out_shape,
        in_specs=[VMEM] * count + [pl.BlockSpec(memory_space=pl.ANY)] * len(after),
        out_specs=[VMEM] * len(out_shape),
        scratch_shapes=scratch,
        compiler_params=pltpu.CompilerParams(vmem_limit_bytes=mib * MIB),
        cost_estimate=cost,
    )(*args, *after)


def tall(rows):
    return [rows[:, start : start + LANES] for start in range(0, rows.shape[1], LANES)]


def put_tall(ref, base, rows):
    count = rows.shape[0]
    for t, piece in enumerate(tall(rows)):
        ref[base + t * count : base + (t + 1) * count, :] = piece


def label_kernel(points_ref, assign_ref, out_ref):
    own_count = points_ref.shape[0]
    assign = assign_ref[...]
    group_of = assign // CL_DEV
    put_tall(out_ref, 0, points_ref[...])
    end = out_ref.shape[0] - ID_ROWS
    out_ref[end:, :] = jnp.zeros((ID_ROWS, LANES), jnp.bfloat16)
    for n, labels in enumerate((group_of, assign - group_of * CL_DEV)):
        out_ref[end:, n * own_count : (n + 1) * own_count] = jnp.broadcast_to(
            labels.astype(jnp.float32), (ID_ROWS, own_count)
        ).astype(jnp.bfloat16)


def select_kernel(slots, *refs):
    *block_refs, local_ref, set_ref, points_ref = refs
    count = len(block_refs)
    points, width = points_ref.shape
    own_count = points // count
    half = count * slots
    me = lax.axis_index("col")
    earlier = (
        lax.broadcasted_iota(jnp.int32, (own_count, own_count), 0)
        < lax.broadcasted_iota(jnp.int32, (own_count, own_count), 1)
    ).astype(jnp.bfloat16)
    slot = lax.broadcasted_iota(jnp.int32, (2 * half, own_count), 0)
    relatives, labels = [], []
    for n, block_ref in enumerate(block_refs):
        for t in range(width // LANES):
            points_ref[n * own_count : (n + 1) * own_count, t * LANES : (t + 1) * LANES] = block_ref[
                t * own_count : (t + 1) * own_count, :
            ]
        end = block_ref.shape[0] - ID_ROWS
        group_of = block_ref[end:, :own_count].astype(jnp.float32).astype(jnp.int32)
        relatives.append(group_of ^ me)
        labels.append(block_ref[end:, own_count : 2 * own_count].astype(jnp.float32) + 1.0)
    members = [
        lax.broadcasted_iota(jnp.int32, (ID_ROWS, own_count), 0) == relative
        for relative in relatives
    ]
    marks = [member.astype(jnp.float32) for member in members]
    ranks = dot(jnp.concatenate(marks, axis=0).astype(jnp.bfloat16), earlier, NN)
    dispatch = []
    for n, (relative, mark) in enumerate(zip(relatives, marks)):
        rank = ranks[n * ID_ROWS : (n + 1) * ID_ROWS] * mark
        position = jnp.sum(rank, axis=0, keepdims=True).astype(jnp.int32)
        target = jnp.where(relative < 2, relative * half + n * slots + position, -1)
        dispatch.append((slot == target[:1]).astype(jnp.bfloat16))
    dispatch = jnp.concatenate(dispatch, axis=1)
    rows = dot(dispatch, points_ref[...], NN).astype(jnp.bfloat16)
    ids = dot(jnp.concatenate(labels, axis=1).astype(jnp.bfloat16), dispatch, NT)
    put_tall(local_ref, 0, points_ref[...])
    for ref, start in ((local_ref, points * width // LANES), (set_ref, 0)):
        end = ref.shape[0] - ID_ROWS
        put_tall(ref, start, rows)
        ref[end:, :] = jnp.zeros((ID_ROWS, LANES), jnp.bfloat16)
        ref[end:, : 2 * half] = ids.astype(jnp.bfloat16)


def column_norms(rows):
    values = rows.astype(jnp.float32)
    return jnp.sum(values * values, axis=1, keepdims=True)


def row_of(column):
    return jnp.transpose(jnp.broadcast_to(column, (column.shape[0], 128)))[:1]


class Half:
    def __init__(self, ref, base, count, second):
        self.ref, self.base, self.count = ref, base, count
        self.start = count if second else 0

    def put(self, out_ref, place):
        for t in range(out_ref.shape[1] // LANES):
            start = self.base + 2 * t * self.count + self.start
            out_ref[place : place + self.count, t * LANES : (t + 1) * LANES] = self.ref[
                start : start + self.count, :
            ]

    def indicator(self, width):
        base = self.base + 2 * self.count * width // LANES
        ids = self.ref[base : base + ID_ROWS, self.start : self.start + self.count]
        ids = ids.astype(jnp.float32).astype(jnp.int32)[:1]
        clusters = lax.broadcasted_iota(jnp.int32, (CL_DEV, self.count), 0)
        return (clusters + 1 == ids).astype(jnp.bfloat16)


def aligned(rows):
    return -(-rows // 16) * 16


def stack_kernel(*refs):
    *in_refs, out_ref = refs
    place = 0
    for in_ref in in_refs:
        out_ref[place : place + in_ref.shape[0], :] = in_ref[...]
        place += aligned(in_ref.shape[0])


def stack(*arrays, cost=None):
    rows = sum(aligned(one.shape[0]) for one in arrays[:-1]) + arrays[-1].shape[0]
    shape = jax.ShapeDtypeStruct((rows, arrays[0].shape[1]), arrays[0].dtype)
    return call(stack_kernel, [shape], arrays, cost=cost)[0]


def kern(rows, slots, slot_norms):
    inner = dot(rows, slots, NT)
    squared = column_norms(rows) + slot_norms - 2.0 * inner
    return jnp.exp(squared * (-1.0 / rows.shape[1])).astype(jnp.bfloat16)


def row_norms(slots_ref):
    pieces = [
        row_of(column_norms(slots_ref[start : start + CL_DEV, :]))
        for start in range(0, slots_ref.shape[0], CL_DEV)
    ]
    return jnp.concatenate(pieces, axis=1)


def chunks(begin, end, step):
    return [(start, min(start + step, end)) for start in range(begin, end, step)]


def sums_kernel(counts, parts, *refs):
    *array_refs, left_ref, hot_ref, sums_ref, totals_ref = refs
    rows, (total, width) = sums_ref.shape[0], left_ref.shape
    place = 0
    for array_ref, count in zip(array_refs, counts):
        for t in range(width // LANES):
            left_ref[place : place + count, t * LANES : (t + 1) * LANES] = array_ref[
                t * count : (t + 1) * count, :
            ]
        place += count
    for n, *rest in parts:
        part = Half(array_refs[n], *rest)
        end = place + part.count
        part.put(left_ref, place)
        hot_ref[:, place - rows : end - rows] = part.indicator(width)
        place = end
    slots, hot = left_ref[rows:, :], hot_ref[...]
    norms = row_norms(left_ref.at[rows:])
    for start, end in chunks(0, rows, 256):
        sums_ref[start:end, :] = dot(kern(left_ref[start:end, :], slots, norms), hot, NT)
    shares = jnp.zeros(hot.shape, jnp.float32)
    for start, end in chunks(rows, total, 256):
        tile = kern(left_ref[start:end, :], slots, norms)
        shares += dot(hot_ref[:, start - rows : end - rows], tile, NN)
    column = jnp.sum(shares * hot.astype(jnp.float32), axis=1, keepdims=True)
    ones = jnp.ones((8, total - rows), jnp.bfloat16)
    totals_ref[:8, :] = jnp.broadcast_to(row_of(column), (8, CL_DEV))
    totals_ref[8:, :] = dot(ones, hot, NT)


def distance_kernel(parts, order, *refs):
    left_ref, old_hot_ref, sums_ref, totals_ref, *refs = refs
    *array_refs, out_ref, slots_ref, hot_ref = refs
    rows, total = sums_ref.shape[0], left_ref.shape[0]
    place = 0
    for n, *rest in parts:
        part = Half(array_refs[n], *rest)
        end = place + part.count
        part.put(slots_ref, place)
        hot_ref[:, place:end] = part.indicator(slots_ref.shape[1])
        place = end
    slots, hot = slots_ref[...], hot_ref[...]
    norms = row_norms(slots_ref)
    whole = kern(left_ref[...], slots, norms) if total * place <= MIB else None

    def tiles(begin, end):
        if whole is not None:
            yield begin, end, whole[begin:end]
            return
        for start, stop in chunks(begin, end, 512):
            yield start, stop, kern(left_ref[start:stop, :], slots, norms)

    shares = dot(hot, kern(slots, slots, norms), NN)
    for start, end, tile in tiles(rows, total):
        shares += 2.0 * dot(old_hot_ref[:, start - rows : end - rows], tile, NN)
    column = jnp.sum(shares * hot.astype(jnp.float32), axis=1, keepdims=True)
    totals = totals_ref[:1, :] + row_of(column)
    counts = totals_ref[8:9, :] + dot(jnp.ones((8, place), jnp.bfloat16), hot, NT)[:1]
    sizes = jnp.maximum(counts, 1.0)
    offset = 1.0 + totals / (sizes * sizes)
    factor = 2.0 / sizes
    me = lax.axis_index("col")
    own_count = rows // len(order)
    for start, end, tile in tiles(0, rows):
        part = offset - (sums_ref[start:end, :] + dot(tile, hot, NT)) * factor
        for b in range((end - start) // own_count):
            row = pl.multiple_of((me ^ order[start // own_count + b]) * own_count, own_count)
            out_ref[pl.ds(row, own_count), :] = part[b * own_count : (b + 1) * own_count]


def parts_of(sets, arrays, width):
    parts = []
    for one, base, count, second in sets:
        n = [array is one for array in arrays].index(True)
        for start in range(base, one.shape[0], aligned(2 * count * width // LANES + ID_ROWS)):
            parts.append((n, start, count, second))
    return parts


def cost_of(rows, slots, width):
    return pl.CostEstimate(
        flops=2 * rows * slots * (width + CL_DEV),
        bytes_accessed=2 * rows * width,
        transcendentals=rows * slots,
    )


def sum_slots(local, sets, width):
    arrays = [one for one, _ in local] + [one for one, base, *_ in sets if not base]
    counts = [base * LANES // width for _, base in local]
    parts = parts_of(sets, arrays, width)
    rows, slots = sum(counts), sum(part[2] for part in parts)
    return call(
        functools.partial(sums_kernel, counts, parts),
        [
            bf16(rows + slots, width),
            bf16(CL_DEV, slots),
            jax.ShapeDtypeStruct((rows, CL_DEV), jnp.float32),
            jax.ShapeDtypeStruct((16, CL_DEV), jnp.float32),
        ],
        arrays,
        mib=32,
        cost=cost_of(1 * (rows + slots), slots, width),
    )


def finish(order, sums, sets, width):
    arrays = [one for one, *_ in sets]
    parts = parts_of(sets, arrays, width)
    slots = sum(part[2] for part in parts)
    return call(
        functools.partial(distance_kernel, parts, order),
        [jax.ShapeDtypeStruct(sums[2].shape, jnp.float32)],
        [*sums, *arrays],
        [pltpu.VMEM((slots, width), jnp.bfloat16), pltpu.VMEM((CL_DEV, slots), jnp.bfloat16)],
        mib=32,
        cost=cost_of(sums[0].shape[0] + slots, slots, width),
    )[0]


def per_device(points, assign):
    own_count, width = points.shape
    group_count, row_count = lax.axis_size("col"), lax.axis_size("row")
    chips, tiles = group_count // 2, width // LANES
    slots = max(2, 2 * own_count // group_count)

    def over_col(values, bits):
        return lax.ppermute(values, "col", [(i, i ^ bits) for i in range(group_count)])

    def over_row(values, bits):
        return lax.ppermute(values, "row", [(i, i ^ bits) for i in range(row_count)])

    def pending(one, flops):
        return stack(one, cost=pl.CostEstimate(flops=int(flops), bytes_accessed=0, transcendentals=0))

    def label(values, ids):
        return call(label_kernel, [bf16(own_count * tiles + ID_ROWS, LANES)], [values, ids])[0]

    assign = assign.reshape(1, own_count)
    far = chips // 2
    blocks = {0: label(points, assign)}
    for q in sorted({far, 1}, reverse=True):
        blocks[q] = label(pending(over_col(points, 2 * q), 1e8 if q > 1 else 4e9), over_col(assign, 2 * q))
    bit = far // 2
    while bit:
        for q in range(0, chips, 2 * bit):
            if q + bit not in blocks:
                blocks[q + bit] = pending(over_col(blocks[q], 2 * bit), 1e9)
        bit //= 2
    places, near, last = [], [], []
    for batch in (range(2), range(2, chips)):
        base, half = len(batch) * own_count * tiles, len(batch) * slots
        set_rows = 2 * half * tiles + ID_ROWS
        here, sets = call(
            functools.partial(select_kernel, slots),
            [bf16(base + set_rows, LANES), bf16(set_rows, LANES)],
            [blocks[q] for q in batch],
            [pltpu.VMEM((len(batch) * own_count, width), jnp.bfloat16)],
            after=[] if last else [blocks[far]],
        )
        got = [over_row(sets, bits) for bits in sorted(range(1, row_count), key=lambda bits: (-bits.bit_count(), bits if last else -bits))]
        places.append([2 * q for q in batch])
        near.append((here, base, half))
        last.append((got, 0, half))

    def both_cores(one, base, half):
        return [(one, base, half, False), (over_col(one, 1), base, half, True)]

    pairs = [both_cores(*one) for one in near]
    local = [pair[side][:2] for side in range(2) for pair in pairs]
    got, base, half = last[0]
    old = [*pairs[0], *both_cores(stack(*got), base, half)]
    order = [q for side in range(2) for batch in places for q in (one ^ side for one in batch)]
    sums = sum_slots(local, old, width)
    got, base, half = last[1]
    return finish(order, sums, [*pairs[1], *both_cores(stack(*got), base, half)], width)


def solution(mesh):
    return jax.shard_map(
        per_device,
        mesh=mesh,
        in_specs=(P(("row", "col"), None), P(("row", "col"))),
        out_specs=P("row", "col"),
        check_vma=False,
    )
```

```python
import functools

import jax
import jax.numpy as jnp
from jax import lax
from jax.experimental import pallas as pl
from jax.experimental.pallas import tpu as pltpu
from jax.sharding import PartitionSpec as P

CL_DEV = 128
ID_ROWS = 8
LANES = 128
NT = (((1,), (1,)), ((), ()))
NN = (((1,), (0,)), ((), ()))
VMEM = pl.BlockSpec(memory_space=pltpu.VMEM)
MIB = 1024 * 1024


def dot(left, right, dims):
    return lax.dot_general(left, right, dims, preferred_element_type=jnp.float32)


def bf16(*shape):
    return jax.ShapeDtypeStruct(shape, jnp.bfloat16)


def call(kernel, out_shape, args, scratch=(), mib=8, after=(), cost=None):
    count = len(args)

    def body(*refs):
        kernel(*refs[:count], *refs[count + len(after) :])

    return pl.pallas_call(
        body,
        out_shape=out_shape,
        in_specs=[VMEM] * count + [pl.BlockSpec(memory_space=pl.ANY)] * len(after),
        out_specs=[VMEM] * len(out_shape),
        scratch_shapes=scratch,
        compiler_params=pltpu.CompilerParams(vmem_limit_bytes=mib * MIB),
        cost_estimate=cost,
    )(*args, *after)


def tall(rows):
    return [rows[:, start : start + LANES] for start in range(0, rows.shape[1], LANES)]


def put_tall(ref, base, rows):
    count = rows.shape[0]
    for t, piece in enumerate(tall(rows)):
        ref[base + t * count : base + (t + 1) * count, :] = piece


def label_kernel(points_ref, assign_ref, out_ref):
    own_count = points_ref.shape[0]
    assign = assign_ref[...]
    group_of = assign // CL_DEV
    put_tall(out_ref, 0, points_ref[...])
    end = out_ref.shape[0] - ID_ROWS
    out_ref[end:, :] = jnp.zeros((ID_ROWS, LANES), jnp.bfloat16)
    for n, labels in enumerate((group_of, assign - group_of * CL_DEV)):
        out_ref[end:, n * own_count : (n + 1) * own_count] = jnp.broadcast_to(
            labels.astype(jnp.float32), (ID_ROWS, own_count)
        ).astype(jnp.bfloat16)


def select_kernel(slots, *refs):
    *block_refs, local_ref, set_ref, points_ref = refs
    count = len(block_refs)
    points, width = points_ref.shape
    own_count = points // count
    half = count * slots
    me = lax.axis_index("col")
    earlier = (
        lax.broadcasted_iota(jnp.int32, (own_count, own_count), 0)
        < lax.broadcasted_iota(jnp.int32, (own_count, own_count), 1)
    ).astype(jnp.bfloat16)
    slot = lax.broadcasted_iota(jnp.int32, (2 * half, own_count), 0)
    relatives, labels = [], []
    for n, block_ref in enumerate(block_refs):
        for t in range(width // LANES):
            points_ref[n * own_count : (n + 1) * own_count, t * LANES : (t + 1) * LANES] = block_ref[
                t * own_count : (t + 1) * own_count, :
            ]
        end = block_ref.shape[0] - ID_ROWS
        group_of = block_ref[end:, :own_count].astype(jnp.float32).astype(jnp.int32)
        relatives.append(group_of ^ me)
        labels.append(block_ref[end:, own_count : 2 * own_count].astype(jnp.float32) + 1.0)
    members = [
        lax.broadcasted_iota(jnp.int32, (ID_ROWS, own_count), 0) == relative
        for relative in relatives
    ]
    marks = [member.astype(jnp.float32) for member in members]
    ranks = dot(jnp.concatenate(marks, axis=0).astype(jnp.bfloat16), earlier, NN)
    dispatch = []
    for n, (relative, mark) in enumerate(zip(relatives, marks)):
        rank = ranks[n * ID_ROWS : (n + 1) * ID_ROWS] * mark
        position = jnp.sum(rank, axis=0, keepdims=True).astype(jnp.int32)
        target = jnp.where(relative < 2, relative * half + n * slots + position, -1)
        dispatch.append((slot == target[:1]).astype(jnp.bfloat16))
    dispatch = jnp.concatenate(dispatch, axis=1)
    rows = dot(dispatch, points_ref[...], NN).astype(jnp.bfloat16)
    ids = dot(jnp.concatenate(labels, axis=1).astype(jnp.bfloat16), dispatch, NT)
    put_tall(local_ref, 0, points_ref[...])
    for ref, start in ((local_ref, points * width // LANES), (set_ref, 0)):
        end = ref.shape[0] - ID_ROWS
        put_tall(ref, start, rows)
        ref[end:, :] = jnp.zeros((ID_ROWS, LANES), jnp.bfloat16)
        ref[end:, : 2 * half] = ids.astype(jnp.bfloat16)


def column_norms(rows):
    values = rows.astype(jnp.float32)
    return jnp.sum(values * values, axis=1, keepdims=True)


def row_of(column):
    return jnp.transpose(jnp.broadcast_to(column, (column.shape[0], 128)))[:1]


class Half:
    def __init__(self, ref, base, count, second):
        self.ref, self.base, self.count = ref, base, count
        self.start = count if second else 0

    def put(self, out_ref, place):
        for t in range(out_ref.shape[1] // LANES):
            start = self.base + 2 * t * self.count + self.start
            out_ref[place : place + self.count, t * LANES : (t + 1) * LANES] = self.ref[
                start : start + self.count, :
            ]

    def indicator(self, width):
        base = self.base + 2 * self.count * width // LANES
        ids = self.ref[base : base + ID_ROWS, self.start : self.start + self.count]
        ids = ids.astype(jnp.float32).astype(jnp.int32)[:1]
        clusters = lax.broadcasted_iota(jnp.int32, (CL_DEV, self.count), 0)
        return (clusters + 1 == ids).astype(jnp.bfloat16)


def aligned(rows):
    return -(-rows // 16) * 16


def stack_kernel(*refs):
    *in_refs, out_ref = refs
    place = 0
    for in_ref in in_refs:
        out_ref[place : place + in_ref.shape[0], :] = in_ref[...]
        place += aligned(in_ref.shape[0])


def stack(*arrays, cost=None):
    rows = sum(aligned(one.shape[0]) for one in arrays[:-1]) + arrays[-1].shape[0]
    shape = jax.ShapeDtypeStruct((rows, arrays[0].shape[1]), arrays[0].dtype)
    return call(stack_kernel, [shape], arrays, cost=cost)[0]


def kern(rows, slots, slot_norms):
    inner = dot(rows, slots, NT)
    squared = column_norms(rows) + slot_norms - 2.0 * inner
    return jnp.exp(squared * (-1.0 / rows.shape[1])).astype(jnp.bfloat16)


def row_norms(slots_ref):
    pieces = [
        row_of(column_norms(slots_ref[start : start + CL_DEV, :]))
        for start in range(0, slots_ref.shape[0], CL_DEV)
    ]
    return jnp.concatenate(pieces, axis=1)


def chunks(begin, end, step):
    return [(start, min(start + step, end)) for start in range(begin, end, step)]


def sums_kernel(counts, parts, *refs):
    *array_refs, left_ref, hot_ref, sums_ref, totals_ref = refs
    rows, (total, width) = sums_ref.shape[0], left_ref.shape
    place = 0
    for array_ref, count in zip(array_refs, counts):
        for t in range(width // LANES):
            left_ref[place : place + count, t * LANES : (t + 1) * LANES] = array_ref[
                t * count : (t + 1) * count, :
            ]
        place += count
    for n, *rest in parts:
        part = Half(array_refs[n], *rest)
        end = place + part.count
        part.put(left_ref, place)
        hot_ref[:, place - rows : end - rows] = part.indicator(width)
        place = end
    slots, hot = left_ref[rows:, :], hot_ref[...]
    norms = row_norms(left_ref.at[rows:])
    for start, end in chunks(0, rows, 512):
        sums_ref[start:end, :] = dot(kern(left_ref[start:end, :], slots, norms), hot, NT)
    shares = jnp.zeros(hot.shape, jnp.float32)
    for start, end in chunks(rows, total, 256):
        tile = kern(left_ref[start:end, :], slots, norms)
        shares += dot(hot_ref[:, start - rows : end - rows], tile, NN)
    column = jnp.sum(shares * hot.astype(jnp.float32), axis=1, keepdims=True)
    ones = jnp.ones((8, total - rows), jnp.bfloat16)
    totals_ref[:8, :] = jnp.broadcast_to(row_of(column), (8, CL_DEV))
    totals_ref[8:, :] = dot(ones, hot, NT)


def distance_kernel(parts, order, *refs):
    left_ref, old_hot_ref, sums_ref, totals_ref, *refs = refs
    *array_refs, out_ref, slots_ref, hot_ref = refs
    rows, total = sums_ref.shape[0], left_ref.shape[0]
    place = 0
    for n, *rest in parts:
        part = Half(array_refs[n], *rest)
        end = place + part.count
        part.put(slots_ref, place)
        hot_ref[:, place:end] = part.indicator(slots_ref.shape[1])
        place = end
    slots, hot = slots_ref[...], hot_ref[...]
    norms = row_norms(slots_ref)
    whole = kern(left_ref[...], slots, norms) if total * place <= MIB else None

    def tiles(begin, end):
        if whole is not None:
            yield begin, end, whole[begin:end]
            return
        for start, stop in chunks(begin, end, 512):
            yield start, stop, kern(left_ref[start:stop, :], slots, norms)

    shares = dot(hot, kern(slots, slots, norms), NN)
    for start, end, tile in tiles(rows, total):
        shares += 2.0 * dot(old_hot_ref[:, start - rows : end - rows], tile, NN)
    column = jnp.sum(shares * hot.astype(jnp.float32), axis=1, keepdims=True)
    totals = totals_ref[:1, :] + row_of(column)
    counts = totals_ref[8:9, :] + dot(jnp.ones((8, place), jnp.bfloat16), hot, NT)[:1]
    sizes = jnp.maximum(counts, 1.0)
    offset = 1.0 + totals / (sizes * sizes)
    factor = 2.0 / sizes
    me = lax.axis_index("col")
    own_count = rows // len(order)
    for start, end, tile in tiles(0, rows):
        part = offset - (sums_ref[start:end, :] + dot(tile, hot, NT)) * factor
        for b in range((end - start) // own_count):
            row = pl.multiple_of((me ^ order[start // own_count + b]) * own_count, own_count)
            out_ref[pl.ds(row, own_count), :] = part[b * own_count : (b + 1) * own_count]


def parts_of(sets, arrays, width):
    parts = []
    for one, base, count, second in sets:
        n = [array is one for array in arrays].index(True)
        for start in range(base, one.shape[0], aligned(2 * count * width // LANES + ID_ROWS)):
            parts.append((n, start, count, second))
    return parts


def cost_of(rows, slots, width):
    return pl.CostEstimate(
        flops=2 * rows * slots * (width + CL_DEV),
        bytes_accessed=2 * rows * width,
        transcendentals=rows * slots,
    )


def sum_slots(local, sets, width):
    arrays = [one for one, _ in local] + [one for one, base, *_ in sets if not base]
    counts = [base * LANES // width for _, base in local]
    parts = parts_of(sets, arrays, width)
    rows, slots = sum(counts), sum(part[2] for part in parts)
    return call(
        functools.partial(sums_kernel, counts, parts),
        [
            bf16(rows + slots, width),
            bf16(CL_DEV, slots),
            jax.ShapeDtypeStruct((rows, CL_DEV), jnp.float32),
            jax.ShapeDtypeStruct((16, CL_DEV), jnp.float32),
        ],
        arrays,
        mib=32,
        cost=cost_of(1 * (rows + slots), slots, width),
    )


def finish(order, sums, sets, width):
    arrays = [one for one, *_ in sets]
    parts = parts_of(sets, arrays, width)
    slots = sum(part[2] for part in parts)
    return call(
        functools.partial(distance_kernel, parts, order),
        [jax.ShapeDtypeStruct(sums[2].shape, jnp.float32)],
        [*sums, *arrays],
        [pltpu.VMEM((slots, width), jnp.bfloat16), pltpu.VMEM((CL_DEV, slots), jnp.bfloat16)],
        mib=32,
        cost=cost_of(sums[0].shape[0] + slots, slots, width),
    )[0]


def per_device(points, assign):
    own_count, width = points.shape
    group_count, row_count = lax.axis_size("col"), lax.axis_size("row")
    chips, tiles = group_count // 2, width // LANES
    slots = max(2, 2 * own_count // group_count)

    def over_col(values, bits):
        return lax.ppermute(values, "col", [(i, i ^ bits) for i in range(group_count)])

    def over_row(values, bits):
        return lax.ppermute(values, "row", [(i, i ^ bits) for i in range(row_count)])

    def pending(one, flops):
        return stack(one, cost=pl.CostEstimate(flops=int(flops), bytes_accessed=0, transcendentals=0))

    def label(values, ids):
        return call(label_kernel, [bf16(own_count * tiles + ID_ROWS, LANES)], [values, ids])[0]

    assign = assign.reshape(1, own_count)
    far = chips // 2
    blocks = {0: label(points, assign)}
    for q in sorted({far, 1}, reverse=True):
        blocks[q] = label(pending(over_col(points, 2 * q), 1e8 if q > 1 else 4e9), over_col(assign, 2 * q))
    bit = far // 2
    while bit:
        for q in range(0, chips, 2 * bit):
            if q + bit not in blocks:
                blocks[q + bit] = pending(over_col(blocks[q], 2 * bit), 1e9)
        bit //= 2
    places, near, last = [], [], []
    for batch in (range(2), range(2, chips)):
        base, half = len(batch) * own_count * tiles, len(batch) * slots
        set_rows = 2 * half * tiles + ID_ROWS
        here, sets = call(
            functools.partial(select_kernel, slots),
            [bf16(base + set_rows, LANES), bf16(set_rows, LANES)],
            [blocks[q] for q in batch],
            [pltpu.VMEM((len(batch) * own_count, width), jnp.bfloat16)],
            after=[] if last else [blocks[far]],
        )
        got = [over_row(sets, bits) for bits in range(row_count - 1, 0, -1)]
        places.append([2 * q for q in batch])
        near.append((here, base, half))
        last.append((got, 0, half))

    def both_cores(one, base, half):
        return [(one, base, half, False), (over_col(one, 1), base, half, True)]

    pairs = [both_cores(*one) for one in near]
    local = [pair[side][:2] for side in range(2) for pair in pairs]
    got, base, half = last[0]
    old = [*pairs[0], *both_cores(stack(*got), base, half)]
    order = [q for side in range(2) for batch in places for q in (one ^ side for one in batch)]
    sums = sum_slots(local, old, width)
    got, base, half = last[1]
    return finish(order, sums, [*pairs[1], *both_cores(stack(*got), base, half)], width)


def solution(mesh):
    return jax.shard_map(
        per_device,
        mesh=mesh,
        in_specs=(P(("row", "col"), None), P(("row", "col"))),
        out_specs=P("row", "col"),
        check_vma=False,
    )
```
